512 devices in a mesh: blk: 8 (over y_lo, x), dp: 64 (over y_hi, z, core).
Axes of the slice: x: 4, y: 4 (y_hi: 2, y_lo: 2; y = y_hi * 2 + y_lo), z: 16, core: 2. Of those that a mesh axis runs over, the one named last changes fastest.
Arguments:
- features: bfloat16 [8, 64, 4, 32, 512], P('blk', 'dp'), may hold values from -16 to 16
- conv_weight: bfloat16 [9, 512, 1024], P(None, None, 'blk'), may hold values from -0.09375 to 0.09375
- projection: bfloat16 [1024, 512], P('blk'), may hold values from -0.1875 to 0.1875
- text: bfloat16 [8, 64, 512], P('blk', 'dp'), may hold values from -6 to 6
- labels: int32 [8, 64], P('blk', 'dp'), may hold values from 0 to 7
Outputs:
- grad_features: bfloat16 [8, 64, 4, 32, 512], P('blk', 'dp')
- grad_weight: float32 [9, 512, 1024], P(None, 'dp', 'blk')
- grad_text: float32 [8, 64, 512], P('blk', 'dp')
The draws below stay inside these ranges and needn't reach their ends.
Inputs may be any that keep to these rules, and one draw needn't show every extreme that they name: labels index the captions of the clip's own group.
All inputs are finite; a program needn't handle non-finite values.
Results may differ from the reference program's by a relative error of at most 0.018.
Values may be sent and summed in bfloat16 or wider, within the bound.
No kernel may reach another device: no remote copies, remote signals or barrier semaphores. Data moves between devices by JAX's collectives and lax.ppermute only.
A program may use at most 64 MiB of HBM per device.

```python
import jax
import jax.numpy as jnp
from jax import lax

CIN = 512
COUT = 1024
EMBED = 512
FREQ = 4
FRAMES = 32
GROUP = 8
GROUPS = 64
N_BLK = 8


def touch_ends(values, own_key, least, largest):
    place = [jax.random.randint(jax.random.fold_in(own_key, axis), (), 0, length) for axis, length in enumerate(values.shape)]
    main_axis = values.shape.index(max(values.shape))
    neighbour = place[:main_axis] + [(place[main_axis] + 1) % values.shape[main_axis]] + place[main_axis + 1:]
    return values.at[tuple(place)].set(least).at[tuple(neighbour)].set(largest)


def spiked(entries, key, source, target, parts, factor):
    def block_of(axis_at):
        return (jnp.arange(entries.shape[axis_at]) // (entries.shape[axis_at] // parts)).reshape((-1,) + (1,) * (entries.ndim - 1 - axis_at))

    one_side = jax.random.permutation(key, parts)[block_of(target)]
    second = (block_of(target) + parts // 2) % parts
    return jnp.where((block_of(source) == one_side) | (block_of(source) == second), factor * entries, entries)


def levels(rng, dims, pieces, least, largest):
    def one(position, parts):
        steps = jax.random.uniform(jax.random.fold_in(jax.random.fold_in(rng, 6), position), (parts,), jnp.float32, least / len(pieces), largest / len(pieces))
        return jnp.repeat(jnp.exp(steps), dims[position] // parts).reshape((-1,) + (1,) * (len(dims) - position - 1))

    gain = one(*pieces[0])
    for cut in pieces[1:]:
        gain = gain * one(*cut)
    return gain


def gaussian(key, shape, spread, limit, split=(), held_as=jnp.bfloat16):
    array = jax.random.normal(key, shape, jnp.float32) * spread
    if len(split) > 0:
        array = levels(key, shape, split, -0.22, 0.18) * array
    return jnp.clip(array, min=-limit, max=limit).astype(held_as)


def bell_draw_with(stream_key, shape, spread, reach, shards, heavy, kind=jnp.bfloat16):
    values = spread * jax.random.normal(stream_key, shape, jnp.float32)
    if shards:
        values = values * levels(stream_key, shape, shards, -0.22, 0.18)
    return jnp.clip(spiked(values, jax.random.fold_in(stream_key, 3), *heavy), -reach, reach).astype(kind)


def setup_inputs(seed: int = 0) -> dict:
    seeds = jax.random.split(jax.random.key(seed), 6)
    return {
        "features": bell_draw_with(seeds[0], (GROUP, GROUPS, FREQ, FRAMES, CIN), 1.0, 16.0, ((0, 8), (1, 64)), (1, 4, 64, 4.0)),
        "conv_weight": gaussian(seeds[1], (9, CIN, COUT), (9 * CIN) ** -0.5, 0.09375, ((2, 8),)),
        "projection": gaussian(seeds[2], (COUT, EMBED), COUT ** -0.5, 0.1875, ((0, 8),)),
        "text": gaussian(seeds[3], (GROUP, GROUPS, EMBED), 1.0, 6.0, ((0, 8), (1, 64))),
        "labels": touch_ends(jax.random.randint(seeds[4], (GROUP, GROUPS), 0, GROUP), jax.random.fold_in(seeds[4], 1), 0, GROUP - 1).astype(jnp.int32),
    }


logit_scale = 10.0
logit_bias = -2.0
loss_scale = 1024.0
norm_eps = 1e-06

def conv_forward(inputs, weights):
    clip_count, freq_bins, frames, _ = inputs.shape
    padded = jnp.pad(inputs, ((0, 0), (1, 1), (1, 1), (0, 0)))
    result = jnp.zeros((clip_count * freq_bins * frames, weights.shape[2]), jnp.float32)
    for row_shift in range(3):
        for col_shift in range(3):
            window = padded[:, col_shift:col_shift + freq_bins, row_shift:row_shift + frames, :]
            window = window.reshape(clip_count * freq_bins * frames, -1)
            result = result + jnp.dot(window, weights[3 * row_shift + col_shift], preferred_element_type=jnp.float32)
    return result.reshape(clip_count, freq_bins, frames, -1)

def weight_gradient(inputs, grads):
    clip_count, freq_bins, frames, _ = inputs.shape
    padded = jnp.pad(inputs, ((0, 0), (1, 1), (1, 1), (0, 0)))
    flat_grads = grads.reshape(clip_count * freq_bins * frames, -1)
    taps = []
    for row_shift in range(3):
        for col_shift in range(3):
            window = padded[:, col_shift:col_shift + freq_bins, row_shift:row_shift + frames, :]
            window = window.reshape(clip_count * freq_bins * frames, -1)
            taps.append(lax.dot_general(window, flat_grads, (((0,), (0,)), ((), ())), preferred_element_type=jnp.float32))
    return jnp.stack(taps)

def input_gradient(grads, weights):
    clip_count, freq_bins, frames, _ = grads.shape
    padded = jnp.pad(grads, ((0, 0), (1, 1), (1, 1), (0, 0)))
    result = jnp.zeros((clip_count * freq_bins * frames, weights.shape[1]), jnp.float32)
    for row_shift in range(3):
        for col_shift in range(3):
            window = padded[:, 2 - col_shift:2 - col_shift + freq_bins, 2 - row_shift:2 - row_shift + frames, :]
            window = window.reshape(clip_count * freq_bins * frames, -1)
            result = result + lax.dot_general(window, weights[3 * row_shift + col_shift], (((1,), (1,)), ((), ())), preferred_element_type=jnp.float32)
    return result.reshape(clip_count, freq_bins, frames, -1)

def silu_slope(values):
    sigma = jax.nn.sigmoid(values)
    return sigma * (1.0 + values * (1.0 - sigma))

def pair_gradient(audio_unit, captions, clip_labels, first_index):
    logits = logit_scale * jnp.dot(audio_unit, captions.T, precision=lax.Precision.HIGHEST) + logit_bias
    columns = first_index + jnp.arange(captions.shape[0], dtype=jnp.int32)
    signs = jnp.where(clip_labels[:, None] == columns[None, :], 1.0, -1.0).astype(logits.dtype)
    return -loss_scale * signs * jax.nn.sigmoid(-signs * logits)

def reference(features, conv_weight, projection, text, labels):
    by_group = jnp.swapaxes(features, 0, 1)
    text_groups = jnp.swapaxes(text, 0, 1)
    label_groups = jnp.swapaxes(labels, 0, 1)
    block_width = COUT // N_BLK
    cell_count = FRAMES * FREQ

    def group_step(weight_sum, inputs):
        clip_features, clip_text, clip_labels = inputs
        preact = conv_forward(clip_features, conv_weight)
        pooled = lax.optimization_barrier(jnp.mean(jax.nn.silu(preact), axis=(1, 2))).astype(jnp.bfloat16)
        embedding = jnp.dot(pooled, projection, preferred_element_type=jnp.float32)
        inv_audio = lax.rsqrt(lax.optimization_barrier(jnp.sum(embedding * embedding, axis=-1, keepdims=True)) + norm_eps)
        audio_unit = embedding * inv_audio
        text_values = clip_text.astype(jnp.float32)
        inv_text = lax.rsqrt(lax.optimization_barrier(jnp.sum(text_values * text_values, axis=-1, keepdims=True)) + norm_eps)
        caption = text_values * inv_text
        pair_grad = pair_gradient(audio_unit, caption, clip_labels, 0)
        audio_grad = logit_scale * jnp.dot(pair_grad, caption, precision=lax.Precision.HIGHEST)
        caption_grad = logit_scale * jnp.dot(pair_grad.T, audio_unit, precision=lax.Precision.HIGHEST)
        grad_text = (caption_grad - caption * lax.optimization_barrier(jnp.sum(caption * caption_grad, axis=-1, keepdims=True))) * inv_text
        embedding_grad = ((audio_grad - audio_unit * lax.optimization_barrier(jnp.sum(audio_unit * audio_grad, axis=-1, keepdims=True))) * inv_audio).astype(jnp.bfloat16)
        pooled_grad = lax.dot_general(embedding_grad, projection, (((1,), (1,)), ((), ())), preferred_element_type=jnp.float32)
        pre_grad = (pooled_grad[:, None, None, :] / cell_count * silu_slope(preact)).astype(jnp.bfloat16)
        feature_sum = jnp.zeros(clip_features.shape, jnp.float32)
        for block_index in range(N_BLK):
            low = block_index * block_width
            partial_value = input_gradient(pre_grad[..., low:low + block_width], conv_weight[..., low:low + block_width])
            feature_sum = feature_sum + lax.optimization_barrier(partial_value.astype(jnp.bfloat16)).astype(jnp.float32)
        weight_sum = weight_sum + weight_gradient(clip_features, pre_grad)
        return (weight_sum, (feature_sum.astype(jnp.bfloat16), grad_text))
    zero_weights = jnp.zeros((9, CIN, COUT), jnp.float32)
    weight_sum, outputs = lax.scan(group_step, zero_weights, (by_group, text_groups, label_groups))
    feature_groups, text_grads = outputs
    return (jnp.swapaxes(feature_groups, 0, 1), weight_sum / GROUPS, jnp.swapaxes(text_grads, 0, 1))
```

```python
import functools

import jax
import jax.numpy as jnp
from jax import lax
from jax.experimental import pallas as pl
from jax.experimental.pallas import tpu as pltpu
from jax.sharding import Mesh, PartitionSpec as P

logit_scale = 10.0
logit_bias = -2.0
loss_scale = 1024.0
norm_eps = 1e-06

BLK = ("ylo", "x")
Z = "z"
f32 = jnp.float32
bf16 = jnp.bfloat16

clips = 8
freq = 4
frames = 32
cells = freq * frames
text_row = cells
label_row = cells + 1
rows = cells + 16
vmem_limit = 48 * 1024 * 1024


def call(kernel, out_shape, scratch=(), flops=0, moved=0):
    return pl.pallas_call(
        kernel,
        out_shape=out_shape,
        scratch_shapes=scratch,
        compiler_params=pltpu.CompilerParams(vmem_limit_bytes=vmem_limit),
        cost_estimate=pl.CostEstimate(flops=flops, bytes_accessed=moved, transcendentals=0),
    )


def frame_index(count):
    return lax.broadcasted_iota(jnp.int32, (count, 1), 0) % frames


def shift_rows(values, step):
    count = values.shape[0]
    frame = frame_index(count)
    if step == 1:
        return jnp.where(frame == 0, 0.0, pltpu.roll(values, 1, 0))
    return jnp.where(frame == frames - 1, 0.0, pltpu.roll(values, count - 1, 0))


def forward_kernel(group_ref, weight_ref, projection_ref, slope_ref, turned_ref, partial_ref):
    inputs = group_ref[:, :cells, :].reshape(clips * cells, -1)
    turned_ref[...] = inputs.T
    out_width = projection_ref.shape[0]
    preact = None
    for a in range(3):
        product = jnp.dot(
            inputs,
            weight_ref[:, 3 * a * out_width : 3 * (a + 1) * out_width],
            preferred_element_type=f32,
        ).reshape(clips, freq, frames, 3 * out_width)
        low = product[..., :out_width]
        mid = product[..., out_width : 2 * out_width]
        high = product[..., 2 * out_width :]
        bins = []
        for f in range(freq):
            total = mid[:, f]
            if f > 0:
                total = total + low[:, f - 1]
            if f < freq - 1:
                total = total + high[:, f + 1]
            bins.append(total[:, None])
        column = jnp.concatenate(bins, axis=1).reshape(clips * cells, out_width)
        if a == 0:
            column = shift_rows(column, 1)
        if a == 2:
            column = shift_rows(column, -1)
        preact = column if preact is None else preact + column
    sigma = jax.nn.sigmoid(preact)
    slope_ref[...] = sigma * (1.0 + preact * (1.0 - sigma))
    active = (preact * sigma).reshape(clips, cells, out_width)
    pooled = (jnp.sum(active, axis=1) * (1.0 / cells)).astype(bf16)
    partial = jnp.dot(pooled, projection_ref[...], preferred_element_type=f32)
    partial_ref[...] = jnp.broadcast_to(partial[None], partial_ref.shape)


def row_sum(values):
    return jnp.sum(values, axis=-1, keepdims=True)


def pair_column(audio_unit, caption_row, clip_labels, column):
    logits = logit_scale * row_sum(audio_unit * caption_row) + logit_bias
    signs = jnp.where(clip_labels == column, 1.0, -1.0)
    return -loss_scale * signs * jax.nn.sigmoid(-signs * logits)


def input_kernel(
    parts_ref, group_ref, slope_ref, weight_ref, projection_ref, feature_ref, text_ref, shifted_ref
):
    embedding = jnp.sum(parts_ref[...], axis=0)
    inv_audio = lax.rsqrt(row_sum(embedding * embedding) + norm_eps)
    audio_unit = embedding * inv_audio
    clip_labels = jnp.concatenate(
        [group_ref[c, cells : cells + 16, :].astype(f32)[1:2, :1] for c in range(clips)], axis=0
    ).astype(jnp.int32)
    position = lax.axis_index("ylo") * 4 + lax.axis_index("x")

    def caption_at(index):
        text_values = group_ref[index, cells : cells + 16, :].astype(f32)[:1]
        inv_text = lax.rsqrt(row_sum(text_values * text_values) + norm_eps)
        return text_values * inv_text, inv_text

    audio_grad = jnp.zeros_like(audio_unit)
    for j in range(clips):
        caption, _ = caption_at(j)
        audio_grad = audio_grad + pair_column(audio_unit, caption, clip_labels, j) * caption
    audio_grad = logit_scale * audio_grad
    caption, inv_text = caption_at(position)
    own_pairs = pair_column(audio_unit, caption, clip_labels, position)
    caption_grad = logit_scale * jnp.sum(own_pairs * audio_unit, axis=0, keepdims=True)
    text_ref[...] = (caption_grad - caption * row_sum(caption * caption_grad)) * inv_text
    embedding_grad = (
        (audio_grad - audio_unit * row_sum(audio_unit * audio_grad)) * inv_audio
    ).astype(bf16)
    pooled_grad = lax.dot_general(
        embedding_grad, projection_ref[...], (((1,), (1,)), ((), ())), preferred_element_type=f32
    )
    width = pooled_grad.shape[1]
    scaled = pooled_grad * (1.0 / cells)
    pre_grad = (scaled[:, None, :] * slope_ref[...].reshape(clips, cells, width)).astype(bf16)
    pre_grad = pre_grad.astype(f32).reshape(clips * cells, width)
    zeros = jnp.zeros((clips, frames, width), bf16)
    for a in range(3):
        moved = pre_grad
        if a == 0:
            moved = shift_rows(pre_grad, -1)
        if a == 2:
            moved = shift_rows(pre_grad, 1)
        moved = moved.astype(bf16).reshape(clips, freq, frames, width)
        for b in range(3):
            tap = 3 * a + b
            for f in range(freq):
                source = f - (b - 1)
                block = moved[:, source] if 0 <= source < freq else zeros
                shifted_ref[:, f, :, tap * width : (tap + 1) * width] = block
    shifted = shifted_ref[...].reshape(clips * cells, -1)
    result = lax.dot_general(
        shifted, weight_ref[...], (((1,), (1,)), ((), ())), preferred_element_type=f32
    )
    feature_ref[...] = result.astype(bf16).reshape(feature_ref.shape)


def weight_kernel(turned_ref, shifted_ref, kept_ref, sent_ref, total_ref):
    width = shifted_ref.shape[-1]
    shifted = shifted_ref[...].reshape(clips * cells, width)
    total_ref[...] = jnp.dot(turned_ref[...], shifted, preferred_element_type=f32).reshape(
        total_ref.shape
    )
    core = lax.axis_index("core")
    kept_ref[...] = total_ref[:, core].reshape(kept_ref.shape)
    sent_ref[...] = total_ref[:, 1 - core].reshape(sent_ref.shape).astype(bf16)


def half_kernel(kept_ref, came_ref, mine_ref, sent_ref, total_ref):
    total_ref[...] = (kept_ref[...] + came_ref[...].astype(f32)).reshape(total_ref.shape)
    side = lax.axis_index("yhi")
    mine_ref[...] = total_ref[side]
    sent_ref[...] = total_ref[1 - side].astype(bf16)


def add_kernel(kept_ref, came_ref, sent_ref):
    sent_ref[...] = (kept_ref[...] + came_ref[...].astype(f32)).astype(bf16)


def final_kernel(group_total, parts_ref, out_ref):
    total = jnp.sum(parts_ref[...].astype(f32), axis=0) * (1.0 / group_total)
    taps, _, width = out_ref.shape
    for tap in range(taps):
        out_ref[tap] = total[:, tap * width : (tap + 1) * width]


def swap(values, axis):
    return lax.ppermute(values, axis, [(0, 1), (1, 0)])


def shards(features, conv_weight, projection, text, labels):
    taps, channels, width = conv_weight.shape
    wide = taps * width
    own = jnp.concatenate(
        [
            features.reshape(cells, channels),
            text.reshape(1, channels),
            jnp.broadcast_to(labels.astype(bf16).reshape(1, 1), (1, channels)),
            jnp.zeros((rows - cells - 2, channels), bf16),
        ]
    )
    weight = jnp.transpose(conv_weight, (1, 0, 2)).reshape(channels, wide)
    group = lax.all_to_all(jnp.broadcast_to(own[None], (clips, rows, channels)), BLK, 0, 0)
    slope, turned, partial = call(
        forward_kernel,
        (
            jax.ShapeDtypeStruct((clips * cells, width), f32),
            jax.ShapeDtypeStruct((channels, clips * cells), bf16),
            jax.ShapeDtypeStruct((clips, clips, projection.shape[1]), f32),
        ),
        flops=2 * clips * cells * channels * wide,
    )(group, weight, projection)
    parts = lax.all_to_all(partial, BLK, 0, 0)
    feature_part, grad_text, shifted = call(
        input_kernel,
        (
            jax.ShapeDtypeStruct((clips, cells, channels), bf16),
            jax.ShapeDtypeStruct((1, channels), f32),
            jax.ShapeDtypeStruct((clips, freq, frames, wide), bf16),
        ),
        flops=2 * clips * cells * channels * wide,
    )(parts, group, slope, weight, projection)
    feature_sum = lax.psum_scatter(feature_part, BLK, scatter_dimension=0, tiled=True)
    half = channels // 2
    quarter = half // 2
    kept, sent = call(
        weight_kernel,
        (jax.ShapeDtypeStruct((half, wide), f32), jax.ShapeDtypeStruct((half, wide), bf16)),
        scratch=[pltpu.VMEM((channels // 16, 2, 8, wide), f32)],
        flops=2 * clips * cells * channels * wide,
    )(turned, shifted)
    came = swap(sent, "core")
    kept, sent = call(
        half_kernel,
        (jax.ShapeDtypeStruct((quarter, wide), f32), jax.ShapeDtypeStruct((quarter, wide), bf16)),
        scratch=[pltpu.VMEM((2, quarter, wide), f32)],
    )(kept, came)
    came = swap(sent, "yhi")
    sent = call(add_kernel, jax.ShapeDtypeStruct((quarter, wide), bf16))(kept, came)
    heights = lax.axis_size(Z)
    parts = lax.all_to_all(sent.reshape(heights, quarter // heights, wide), Z, 0, 0)
    group_total = heights * 4
    grad_weight = call(
        functools.partial(final_kernel, group_total),
        jax.ShapeDtypeStruct((taps, quarter // heights, width), f32),
    )(parts)
    grad_features = feature_sum.reshape(features.shape)
    return (grad_features, grad_weight, grad_text.reshape(1, 1, channels))


def solution(mesh):
    fine = Mesh(mesh.devices.reshape(2, 4, 2, 16, 2), ("ylo", "x", "yhi", "z", "core"))
    dp = ("yhi", "z", "core")
    placed = (
        P(BLK, dp, None, None, None),
        P(None, None, BLK),
        P(BLK, None),
        P(BLK, dp, None),
        P(BLK, dp),
    )
    return jax.shard_map(
        shards,
        mesh=fine,
        in_specs=placed,
        out_specs=(P(BLK, dp, None, None, None), P(None, dp, BLK), P(BLK, dp, None)),
        check_vma=False,
    )
```

```python
import functools

import jax
import jax.numpy as jnp
from jax import lax
from jax.experimental import pallas as pl
from jax.experimental.pallas import tpu as pltpu
from jax.sharding import Mesh, PartitionSpec as P

logit_scale = 10.0
logit_bias = -2.0
loss_scale = 1024.0
norm_eps = 1e-06

BLK = ("ylo", "x")
Z = "z"
f32 = jnp.float32
bf16 = jnp.bfloat16

clips = 8
freq = 4
frames = 32
cells = freq * frames
columns = 4
vmem_limit = 40 * 1024 * 1024
HBM = pl.BlockSpec(memory_space=pltpu.HBM)
VMEM = pl.BlockSpec(memory_space=pltpu.VMEM)
DMA = pltpu.SemaphoreType.DMA


def shape(dims, dtype):
    return jax.ShapeDtypeStruct(dims, dtype)


def call(kernel, out_shape, scratch=(), flops=0, **specs):
    return pl.pallas_call(
        kernel,
        out_shape=out_shape,
        scratch_shapes=scratch,
        compiler_params=pltpu.CompilerParams(vmem_limit_bytes=vmem_limit),
        cost_estimate=pl.CostEstimate(flops=flops, bytes_accessed=0, transcendentals=0),
        **specs,
    )


def copy_kernel(own_ref, out_ref, sems):
    copies = [
        pltpu.make_async_copy(own_ref.at[0], out_ref.at[c], sems.at[c]) for c in range(clips)
    ]
    for copy in copies:
        copy.start()
    for copy in copies:
        copy.wait()


def frame_index(count):
    return lax.broadcasted_iota(jnp.int32, (count, 1), 0) % frames


def shift_rows(values, step):
    count = values.shape[0]
    frame = frame_index(count)
    if step == 1:
        return jnp.where(frame == 0, 0.0, pltpu.roll(values, 1, 0))
    return jnp.where(frame == frames - 1, 0.0, pltpu.roll(values, count - 1, 0))


def forward_kernel(
    group_ref,
    weight_ref,
    projection_ref,
    caption_ref,
    label_ref,
    slope_ref,
    partial_ref,
    slope_buf,
    slope_sem,
):
    inputs = group_ref[...].reshape(clips * cells, -1)
    out_width = projection_ref.shape[0]
    preact = None
    for a in range(3):
        product = jnp.dot(
            inputs,
            weight_ref[:, 3 * a * out_width : 3 * (a + 1) * out_width],
            preferred_element_type=f32,
        ).reshape(clips, freq, frames, 3 * out_width)
        low = product[..., :out_width]
        mid = product[..., out_width : 2 * out_width]
        high = product[..., 2 * out_width :]
        bins = []
        for f in range(freq):
            total = mid[:, f]
            if f > 0:
                total = total + low[:, f - 1]
            if f < freq - 1:
                total = total + high[:, f + 1]
            bins.append(total[:, None])
        column = jnp.concatenate(bins, axis=1).reshape(clips * cells, out_width)
        if a == 0:
            column = shift_rows(column, 1)
        if a == 2:
            column = shift_rows(column, -1)
        preact = column if preact is None else preact + column
    sigma = jax.nn.sigmoid(preact)
    slope_buf[...] = sigma * (1.0 + preact * (1.0 - sigma))
    slope_copy = pltpu.make_async_copy(slope_buf, slope_ref, slope_sem)
    slope_copy.start()
    active = (preact * sigma).reshape(clips, cells, out_width)
    pooled = (jnp.sum(active, axis=1) * (1.0 / cells)).astype(bf16)
    partial = jnp.dot(pooled, projection_ref[...], preferred_element_type=f32)
    embed = partial.shape[1]
    partial_ref[:, :, :embed] = jnp.broadcast_to(partial[None], (clips, clips, embed))
    own_caption = caption_ref[...].astype(f32)
    lanes = partial_ref.shape[2] - embed
    for piece in range(embed // lanes):
        part = own_caption[:, piece * lanes : (piece + 1) * lanes]
        partial_ref[:, piece : piece + 1, embed:] = jnp.broadcast_to(
            part[None], (clips, 1, lanes)
        )
    label = jnp.full((clips, clips // 2, lanes), label_ref[0, 0], jnp.int32)
    partial_ref[:, clips // 2 :, embed:] = label.astype(f32)
    slope_copy.wait()


def turn_kernel(group_ref, turned_ref):
    channels = group_ref.shape[-1]
    inputs = group_ref[...].reshape(clips * cells, channels)
    target = lax.broadcasted_iota(jnp.int32, (channels, channels), 0)
    source = lax.broadcasted_iota(jnp.int32, (channels, channels), 1)
    half = channels // 2
    core = target // half
    within = target - core * half
    wanted = ((within // 8) * 2 + core) * 8 + within % 8
    order = jnp.where(source == wanted, 1.0, 0.0).astype(bf16)
    turned = lax.dot_general(
        order, inputs, (((1,), (1,)), ((), ())), preferred_element_type=f32
    )
    turned_ref[...] = turned.astype(bf16).reshape(turned_ref.shape)


def row_sum(values):
    return jnp.sum(values, axis=-1, keepdims=True)


def pair_column(audio_unit, caption_row, clip_labels, column):
    logits = logit_scale * row_sum(audio_unit * caption_row) + logit_bias
    signs = jnp.where(clip_labels == column, 1.0, -1.0)
    return -loss_scale * signs * jax.nn.sigmoid(-signs * logits)


def pair_kernel(
    parts_ref,
    slope_ref,
    projection_ref,
    turned_ref,
    text_ref,
    shifted_ref,
    sent_ref,
    slope_buf,
    projection_buf,
    turned_buf,
    sems,
):
    core = lax.axis_index("core")
    copies = [
        pltpu.make_async_copy(projection_ref, projection_buf, sems.at[0]),
        pltpu.make_async_copy(slope_ref, slope_buf, sems.at[1]),
        pltpu.make_async_copy(turned_ref.at[1 - core], turned_buf, sems.at[2]),
    ]
    for copy in copies:
        copy.start()
    embed = projection_ref.shape[1]
    lanes = parts_ref.shape[2] - embed
    embedding = jnp.sum(parts_ref[:, :, :embed], axis=0)
    inv_audio = lax.rsqrt(row_sum(embedding * embedding) + norm_eps)
    audio_unit = embedding * inv_audio
    clip_labels = jnp.concatenate(
        [parts_ref[c, clips - 1 :, embed : embed + 1] for c in range(clips)], axis=0
    ).astype(jnp.int32)
    position = lax.axis_index("ylo") * columns + lax.axis_index("x")

    def caption_at(index):
        text_values = jnp.concatenate(
            [parts_ref[index, p : p + 1, embed:] for p in range(embed // lanes)], axis=1
        )
        inv_text = lax.rsqrt(row_sum(text_values * text_values) + norm_eps)
        return text_values * inv_text, inv_text

    audio_grad = jnp.zeros_like(audio_unit)
    for j in range(clips):
        caption, _ = caption_at(j)
        audio_grad = audio_grad + pair_column(audio_unit, caption, clip_labels, j) * caption
    audio_grad = logit_scale * audio_grad
    caption, inv_text = caption_at(position)
    own_pairs = pair_column(audio_unit, caption, clip_labels, position)
    caption_grad = logit_scale * jnp.sum(own_pairs * audio_unit, axis=0, keepdims=True)
    text_ref[...] = (caption_grad - caption * row_sum(caption * caption_grad)) * inv_text
    embedding_grad = (
        (audio_grad - audio_unit * row_sum(audio_unit * audio_grad)) * inv_audio
    ).astype(bf16)
    copies[0].wait()
    pooled_grad = lax.dot_general(
        embedding_grad, projection_buf[...], (((1,), (1,)), ((), ())), preferred_element_type=f32
    )
    width = pooled_grad.shape[1]
    scaled = pooled_grad * (1.0 / cells)
    copies[1].wait()
    pre_grad = (scaled[:, None, :] * slope_buf[...].reshape(clips, cells, width)).astype(bf16)
    pre_grad = pre_grad.astype(f32).reshape(clips * cells, width)
    zeros = jnp.zeros((clips, frames, width), bf16)
    for a in range(3):
        moved = pre_grad
        if a == 0:
            moved = shift_rows(pre_grad, -1)
        if a == 2:
            moved = shift_rows(pre_grad, 1)
        moved = moved.astype(bf16).reshape(clips, freq, frames, width)
        for b in range(3):
            tap = 3 * a + b
            for f in range(freq):
                source = f - (b - 1)
                block = moved[:, source] if 0 <= source < freq else zeros
                shifted_ref[:, f, :, tap * width : (tap + 1) * width] = block
    shifted = shifted_ref[...].reshape(clips * cells, -1)
    copies[2].wait()
    sent_ref[...] = jnp.dot(turned_buf[...], shifted, preferred_element_type=f32).astype(bf16)


def keep_kernel(turned_ref, shifted_ref, kept_ref, turned_buf, sem):
    core = lax.axis_index("core")
    copy = pltpu.make_async_copy(turned_ref.at[core], turned_buf, sem)
    copy.start()
    copy.wait()
    shifted = shifted_ref[...].reshape(clips * cells, -1)
    kept_ref[...] = jnp.dot(turned_buf[...], shifted, preferred_element_type=f32)


def half_kernel(kept_ref, came_ref, mine_ref, sent_ref, total_ref):
    total_ref[...] = (kept_ref[...] + came_ref[...].astype(f32)).reshape(total_ref.shape)
    side = lax.axis_index("yhi")
    mine_ref[...] = total_ref[side]
    sent_ref[...] = total_ref[1 - side].astype(bf16)


def input_kernel(shifted_ref, weight_ref, after_ref, *rest):
    out_refs, total_ref = rest[:columns], rest[columns]
    shifted = shifted_ref[...].reshape(clips * cells, -1)
    result = lax.dot_general(
        shifted, weight_ref[...], (((1,), (1,)), ((), ())), preferred_element_type=f32
    )
    total_ref[...] = result.astype(bf16).reshape(total_ref.shape)
    here = lax.axis_index("x")
    for d in range(columns):
        out_refs[d][...] = total_ref[:, here ^ d]


def add_kernel(kept_ref, came_ref, after_ref, sent_ref, sent_buf, sem):
    sent_buf[...] = (kept_ref[...] + came_ref[...].astype(f32)).astype(bf16)
    copy = pltpu.make_async_copy(sent_buf, sent_ref, sem)
    copy.start()
    copy.wait()


def column_kernel(own_ref, a_ref, b_ref, c_ref, mine_ref, sent_ref, total_ref):
    total = own_ref[...].astype(f32)
    for ref in (a_ref, b_ref, c_ref):
        total = total + ref[...].astype(f32)
    total_ref[...] = total
    side = lax.axis_index("ylo")
    mine_ref[...] = total_ref[side]
    sent_ref[...] = total_ref[1 - side].astype(bf16)


def join_kernel(mine_ref, came_ref, out_ref):
    out_ref[...] = (mine_ref[...] + came_ref[...].astype(f32)).astype(bf16)


def final_kernel(group_total, parts_ref, out_ref):
    total = jnp.sum(parts_ref[...].astype(f32), axis=0) * (1.0 / group_total)
    taps, _, width = out_ref.shape
    for tap in range(taps):
        out_ref[tap] = total[:, tap * width : (tap + 1) * width]


def swap(values, axis):
    return lax.ppermute(values, axis, [(0, 1), (1, 0)])


def shards(features, conv_weight, projection, text, labels):
    taps, channels, width = conv_weight.shape
    wide = taps * width
    embed = projection.shape[1]
    half = channels // 2
    quarter = half // 2
    matmul = 2 * clips * cells * channels * wide
    weight = jnp.transpose(conv_weight, (1, 0, 2)).reshape(channels, wide)
    copies = call(
        copy_kernel,
        shape((clips, cells, channels), bf16),
        scratch=[DMA((clips,))],
        in_specs=[HBM],
        out_specs=HBM,
    )(features.reshape(1, cells, channels))
    group = lax.all_to_all(copies, BLK, 0, 0)
    slope, partial = call(
        forward_kernel,
        (shape((clips * cells, width), f32), shape((clips, clips, embed + 128), f32)),
        scratch=[pltpu.VMEM((clips * cells, width), f32), DMA],
        out_specs=(HBM, VMEM),
        flops=matmul,
    )(group, weight, projection, text.reshape(1, embed), labels)
    parts = lax.all_to_all(partial, BLK, 0, 0)
    turned = call(turn_kernel, shape((2, half, clips * cells), bf16), flops=matmul // 4)(group)
    grad_text, shifted, sent = call(
        pair_kernel,
        (
            shape((1, embed), f32),
            shape((clips, freq, frames, wide), bf16),
            shape((half, wide), bf16),
        ),
        scratch=[
            pltpu.VMEM((clips * cells, width), f32),
            pltpu.VMEM(projection.shape, bf16),
            pltpu.VMEM((half, clips * cells), bf16),
            DMA((3,)),
        ],
        in_specs=[VMEM, HBM, HBM, HBM],
        flops=matmul // 2,
    )(parts, slope, projection, turned)
    kept = call(
        keep_kernel,
        shape((half, wide), f32),
        scratch=[pltpu.VMEM((half, clips * cells), bf16), DMA],
        in_specs=[HBM, VMEM],
        flops=matmul // 2,
    )(turned, shifted)
    came = swap(sent, "core")
    kept, sent = call(
        half_kernel,
        (shape((quarter, wide), f32), shape((quarter, wide), bf16)),
        scratch=[pltpu.VMEM((2, quarter, wide), f32)],
    )(kept, came)
    columns_out = call(
        input_kernel,
        tuple(shape((2, cells, channels), bf16) for _ in range(columns)),
        scratch=[pltpu.VMEM((2, columns, cells, channels), bf16)],
        in_specs=[VMEM, VMEM, pl.BlockSpec(memory_space=pl.ANY)],
        flops=matmul,
    )(shifted, weight, kept)
    came = swap(sent, "yhi")
    sent = call(
        add_kernel,
        shape((quarter, wide), bf16),
        scratch=[pltpu.VMEM((quarter, wide), bf16), DMA],
        in_specs=[VMEM, VMEM, pl.BlockSpec(memory_space=pl.ANY)],
        out_specs=HBM,
    )(kept, came, columns_out[0])
    heights = lax.axis_size(Z)
    parts = lax.all_to_all(sent.reshape(heights, quarter // heights, wide), Z, 0, 0)
    others = [
        lax.ppermute(columns_out[d], "x", [(i, i ^ d) for i in range(columns)])
        for d in range(1, columns)
    ]
    mine, other = call(
        column_kernel,
        (shape((cells, channels), f32), shape((cells, channels), bf16)),
        scratch=[pltpu.VMEM((2, cells, channels), f32)],
        flops=int(1e10),
    )(columns_out[0], *others)
    grad_features = call(join_kernel, shape((cells, channels), bf16))(mine, swap(other, "ylo"))
    grad_weight = call(
        functools.partial(final_kernel, heights * 4),
        shape((taps, quarter // heights, width), f32),
    )(parts)
    return (
        grad_features.reshape(features.shape),
        grad_weight,
        grad_text.reshape(1, 1, embed),
    )


def solution(mesh):
    fine = Mesh(mesh.devices.reshape(2, columns, 2, 16, 2), ("ylo", "x", "yhi", "z", "core"))
    dp = ("yhi", "z", "core")
    placed = (
        P(BLK, dp, None, None, None),
        P(None, None, BLK),
        P(BLK, None),
        P(BLK, dp, None),
        P(BLK, dp),
    )
    return jax.shard_map(
        shards,
        mesh=fine,
        in_specs=placed,
        out_specs=(P(BLK, dp, None, None, None), P(None, dp, BLK), P(BLK, dp, None)),
        check_vma=False,
    )
```

```python
import functools

import jax
import jax.numpy as jnp
from jax import lax
from jax.experimental import pallas as pl
from jax.experimental.pallas import tpu as pltpu
from jax.sharding import Mesh, PartitionSpec as P

logit_scale = 10.0
logit_bias = -2.0
loss_scale = 1024.0
norm_eps = 1e-06

BLK = ("ylo", "x")
Z = "z"
f32 = jnp.float32
bf16 = jnp.bfloat16

clips = 8
freq = 4
frames = 32
cells = freq * frames
columns = 4
vmem_limit = 40 * 1024 * 1024
HBM = pl.BlockSpec(memory_space=pltpu.HBM)
VMEM = pl.BlockSpec(memory_space=pltpu.VMEM)
DMA = pltpu.SemaphoreType.DMA


def shape(dims, dtype):
    return jax.ShapeDtypeStruct(dims, dtype)


def call(kernel, out_shape, scratch=(), flops=0, **specs):
    return pl.pallas_call(
        kernel,
        out_shape=out_shape,
        scratch_shapes=scratch,
        compiler_params=pltpu.CompilerParams(vmem_limit_bytes=vmem_limit),
        cost_estimate=pl.CostEstimate(flops=flops, bytes_accessed=0, transcendentals=0),
        **specs,
    )


def copy_kernel(own_ref, given_ref, copies_ref, extra_ref):
    copies_ref[...] = jnp.broadcast_to(own_ref[...][None], copies_ref.shape)
    extra_ref[...] = given_ref[...]


def frame_index(count):
    return lax.broadcasted_iota(jnp.int32, (count, 1), 0) % frames


def shift_rows(values, step):
    count = values.shape[0]
    frame = frame_index(count)
    if step == 1:
        return jnp.where(frame == 0, 0.0, pltpu.roll(values, 1, 0))
    return jnp.where(frame == frames - 1, 0.0, pltpu.roll(values, count - 1, 0))


def forward_kernel(
    group_ref,
    weight_ref,
    projection_ref,
    extra_ref,
    slope_ref,
    turned_ref,
    partial_ref,
):
    inputs = group_ref[...].reshape(clips * cells, -1)
    turned = inputs.T.astype(f32).reshape(-1, 2, 8, clips * cells)
    for core in range(2):
        turned_ref[core] = turned[:, core].reshape(turned_ref.shape[1:]).astype(bf16)
    out_width = projection_ref.shape[0]
    preact = None
    for a in range(3):
        product = jnp.dot(
            inputs,
            jnp.concatenate([weight_ref[3 * a + b] for b in range(3)], axis=1),
            preferred_element_type=f32,
        ).reshape(clips, freq, frames, 3 * out_width)
        low = product[..., :out_width]
        mid = product[..., out_width : 2 * out_width]
        high = product[..., 2 * out_width :]
        bins = []
        for f in range(freq):
            total = mid[:, f]
            if f > 0:
                total = total + low[:, f - 1]
            if f < freq - 1:
                total = total + high[:, f + 1]
            bins.append(total[:, None])
        column = jnp.concatenate(bins, axis=1).reshape(clips * cells, out_width)
        if a == 0:
            column = shift_rows(column, 1)
        if a == 2:
            column = shift_rows(column, -1)
        preact = column if preact is None else preact + column
    sigma = jax.nn.sigmoid(preact)
    slope_ref[...] = sigma * (1.0 + preact * (1.0 - sigma))
    active = (preact * sigma).reshape(clips, cells, out_width)
    pooled = (jnp.sum(active, axis=1) * (1.0 / cells)).astype(bf16)
    partial = jnp.dot(pooled, projection_ref[...], preferred_element_type=f32)
    embed = partial.shape[1]
    partial_ref[:, :, :embed] = jnp.broadcast_to(partial[None], (clips, clips, embed))
    partial_ref[:, :, embed:] = jnp.broadcast_to(
        extra_ref[...][None], (clips, clips, extra_ref.shape[1])
    )


def row_sum(values):
    return jnp.sum(values, axis=-1, keepdims=True)


def pair_column(audio_unit, caption_row, clip_labels, column):
    logits = logit_scale * row_sum(audio_unit * caption_row) + logit_bias
    signs = jnp.where(clip_labels == column, 1.0, -1.0)
    return -loss_scale * signs * jax.nn.sigmoid(-signs * logits)


def pair_kernel(
    parts_ref,
    slope_ref,
    projection_ref,
    turned_ref,
    text_ref,
    shifted_ref,
    sent_ref,
):
    core = lax.axis_index("core")
    embed = projection_ref.shape[1]
    lanes = parts_ref.shape[2] - embed
    embedding = jnp.sum(parts_ref[:, :, :embed], axis=0)
    inv_audio = lax.rsqrt(row_sum(embedding * embedding) + norm_eps)
    audio_unit = embedding * inv_audio
    clip_labels = jnp.concatenate(
        [parts_ref[c, clips - 1 :, embed : embed + 1] for c in range(clips)], axis=0
    ).astype(jnp.int32)
    position = lax.axis_index("ylo") * columns + lax.axis_index("x")

    def caption_at(index):
        text_values = jnp.concatenate(
            [parts_ref[index, p : p + 1, embed:] for p in range(embed // lanes)], axis=1
        )
        inv_text = lax.rsqrt(row_sum(text_values * text_values) + norm_eps)
        return text_values * inv_text, inv_text

    audio_grad = jnp.zeros_like(audio_unit)
    for j in range(clips):
        caption, _ = caption_at(j)
        audio_grad = audio_grad + pair_column(audio_unit, caption, clip_labels, j) * caption
    audio_grad = logit_scale * audio_grad
    caption, inv_text = caption_at(position)
    own_pairs = pair_column(audio_unit, caption, clip_labels, position)
    caption_grad = logit_scale * jnp.sum(own_pairs * audio_unit, axis=0, keepdims=True)
    text_ref[...] = (caption_grad - caption * row_sum(caption * caption_grad)) * inv_text
    embedding_grad = (
        (audio_grad - audio_unit * row_sum(audio_unit * audio_grad)) * inv_audio
    ).astype(bf16)
    pooled_grad = lax.dot_general(
        embedding_grad, projection_ref[...], (((1,), (1,)), ((), ())), preferred_element_type=f32
    )
    width = pooled_grad.shape[1]
    scaled = pooled_grad * (1.0 / cells)
    pre_grad = (scaled[:, None, :] * slope_ref[...].reshape(clips, cells, width)).astype(bf16)
    pre_grad = pre_grad.astype(f32).reshape(clips * cells, width)
    zeros = jnp.zeros((clips, frames, width), bf16)
    for a in range(3):
        moved = pre_grad
        if a == 0:
            moved = shift_rows(pre_grad, -1)
        if a == 2:
            moved = shift_rows(pre_grad, 1)
        moved = moved.astype(bf16).reshape(clips, freq, frames, width)
        for b in range(3):
            tap = 3 * a + b
            for f in range(freq):
                source = f - (b - 1)
                block = moved[:, source] if 0 <= source < freq else zeros
                shifted_ref[:, f, :, tap * width : (tap + 1) * width] = block
    shifted = shifted_ref[...].reshape(clips * cells, -1)
    sent_ref[...] = jnp.dot(turned_ref[1 - core], shifted, preferred_element_type=f32).astype(bf16)


def keep_kernel(turned_ref, shifted_ref, kept_ref):
    core = lax.axis_index("core")
    shifted = shifted_ref[...].reshape(clips * cells, -1)
    kept_ref[...] = jnp.dot(turned_ref[core], shifted, preferred_element_type=f32)


def half_kernel(kept_ref, came_ref, mine_ref, sent_ref, total_ref):
    total_ref[...] = (kept_ref[...] + came_ref[...].astype(f32)).reshape(total_ref.shape)
    side = lax.axis_index("yhi")
    mine_ref[...] = total_ref[side]
    sent_ref[...] = total_ref[1 - side].astype(bf16)


def input_kernel(shifted_ref, weight_ref, after_ref, *rest):
    out_refs, total_ref = rest[:columns], rest[columns]
    shifted = shifted_ref[...].reshape(clips * cells, -1)
    weight = jnp.concatenate([weight_ref[tap] for tap in range(weight_ref.shape[0])], axis=1)
    result = lax.dot_general(
        shifted, weight, (((1,), (1,)), ((), ())), preferred_element_type=f32
    )
    total_ref[...] = result.astype(bf16).reshape(total_ref.shape)
    here = lax.axis_index("x")
    for d in range(columns):
        out_refs[d][...] = total_ref[:, here ^ d]


def add_kernel(kept_ref, came_ref, after_ref, sent_ref, sent_buf, sem):
    sent_buf[...] = (kept_ref[...] + came_ref[...].astype(f32)).astype(bf16)
    copy = pltpu.make_async_copy(sent_buf, sent_ref, sem)
    copy.start()
    copy.wait()


def near_kernel(own_ref, a_ref, b_ref, total_ref):
    total_ref[...] = own_ref[...].astype(f32) + a_ref[...].astype(f32) + b_ref[...].astype(f32)


def column_kernel(near_ref, c_ref, mine_ref, sent_ref, total_ref):
    total_ref[...] = near_ref[...] + c_ref[...].astype(f32)
    side = lax.axis_index("ylo")
    mine_ref[...] = total_ref[side]
    sent_ref[...] = total_ref[1 - side].astype(bf16)


def join_kernel(mine_ref, came_ref, out_ref):
    out_ref[...] = (mine_ref[...] + came_ref[...].astype(f32)).astype(bf16)


def final_kernel(group_total, parts_ref, out_ref):
    total = jnp.sum(parts_ref[...].astype(f32), axis=0) * (1.0 / group_total)
    taps, _, width = out_ref.shape
    for tap in range(taps):
        out_ref[tap] = total[:, tap * width : (tap + 1) * width]


def swap(values, axis):
    return lax.ppermute(values, axis, [(0, 1), (1, 0)])


def shards(features, conv_weight, projection, text, labels):
    taps, channels, width = conv_weight.shape
    wide = taps * width
    embed = projection.shape[1]
    half = channels // 2
    quarter = half // 2
    matmul = 2 * clips * cells * channels * wide
    given = jnp.concatenate(
        [
            text.reshape(4, embed // 4).astype(f32),
            jnp.broadcast_to(labels.astype(f32), (4, embed // 4)),
        ]
    )
    copies, extra = call(
        copy_kernel, (shape((clips, cells, channels), bf16), shape(given.shape, f32))
    )(features.reshape(cells, channels), given)
    group = lax.all_to_all(copies, BLK, 0, 0)
    slope, turned, partial = call(
        forward_kernel,
        (
            shape((clips * cells, width), f32),
            shape((2, half, clips * cells), bf16),
            shape((clips, clips, embed + 128), f32),
        ),
        flops=matmul,
    )(group, conv_weight, projection, extra)
    parts = lax.all_to_all(partial, BLK, 0, 0)
    grad_text, shifted, sent = call(
        pair_kernel,
        (
            shape((1, embed), f32),
            shape((clips, freq, frames, wide), bf16),
            shape((half, wide), bf16),
        ),
        flops=matmul // 2,
    )(parts, slope, projection, turned)
    kept = call(
        keep_kernel,
        shape((half, wide), f32),
        flops=matmul // 2,
    )(turned, shifted)
    came = swap(sent, "core")
    kept, sent = call(
        half_kernel,
        (shape((quarter, wide), f32), shape((quarter, wide), bf16)),
        scratch=[pltpu.VMEM((2, quarter, wide), f32)],
    )(kept, came)
    columns_out = call(
        input_kernel,
        tuple(shape((2, cells, channels), bf16) for _ in range(columns)),
        scratch=[pltpu.VMEM((2, columns, cells, channels), bf16)],
        in_specs=[VMEM, VMEM, pl.BlockSpec(memory_space=pl.ANY)],
        flops=matmul,
    )(shifted, conv_weight, kept)
    came = swap(sent, "yhi")
    sent = call(
        add_kernel,
        shape((quarter, wide), bf16),
        scratch=[pltpu.VMEM((quarter, wide), bf16), DMA],
        in_specs=[VMEM, VMEM, pl.BlockSpec(memory_space=pl.ANY)],
        out_specs=HBM,
    )(kept, came, columns_out[0])
    heights = lax.axis_size(Z)
    parts = lax.all_to_all(sent.reshape(heights, quarter // heights, wide), Z, 0, 0)
    others = [
        lax.ppermute(columns_out[d], "x", [(i, i ^ d) for i in range(columns)])
        for d in range(1, columns)
    ]
    near = call(near_kernel, shape((2, cells, channels), f32), flops=int(1e10))(
        columns_out[0], others[0], others[2]
    )
    mine, other = call(
        column_kernel,
        (shape((cells, channels), f32), shape((cells, channels), bf16)),
        scratch=[pltpu.VMEM((2, cells, channels), f32)],
        flops=int(0),
    )(near, others[1])
    grad_features = call(join_kernel, shape((cells, channels), bf16))(mine, swap(other, "ylo"))
    grad_weight = call(
        functools.partial(final_kernel, heights * 4),
        shape((taps, quarter // heights, width), f32),
    )(parts)
    return (
        grad_features.reshape(features.shape),
        grad_weight,
        grad_text.reshape(1, 1, embed),
    )


def solution(mesh):
    fine = Mesh(mesh.devices.reshape(2, columns, 2, 16, 2), ("ylo", "x", "yhi", "z", "core"))
    dp = ("yhi", "z", "core")
    placed = (
        P(BLK, dp, None, None, None),
        P(None, None, BLK),
        P(BLK, None),
        P(BLK, dp, None),
        P(BLK, dp),
    )
    return jax.shard_map(
        shards,
        mesh=fine,
        in_specs=placed,
        out_specs=(P(BLK, dp, None, None, None), P(None, dp, BLK), P(BLK, dp, None)),
        check_vma=False,
    )
```

```python
import functools

import jax
import jax.numpy as jnp
from jax import lax
from jax.experimental import pallas as pl
from jax.experimental.pallas import tpu as pltpu
from jax.sharding import Mesh, PartitionSpec as P

logit_scale = 10.0
logit_bias = -2.0
loss_scale = 1024.0
norm_eps = 1e-06

BLK = ("ylo", "x")
NEAR = ("yhi", "zl")
FAR = "z8"
f32 = jnp.float32
bf16 = jnp.bfloat16

clips = 8
freq = 4
frames = 32
cells = freq * frames
columns = 4
heights = 8
first_far = 4
far_order = [(first_far + p) % heights for p in range(heights)]
vmem_limit = 40 * 1024 * 1024
HBM = pl.BlockSpec(memory_space=pltpu.HBM)
VMEM = pl.BlockSpec(memory_space=pltpu.VMEM)
DMA = pltpu.SemaphoreType.DMA


def shape(dims, dtype):
    return jax.ShapeDtypeStruct(dims, dtype)


def call(kernel, out_shape, scratch=(), flops=0, **specs):
    return pl.pallas_call(
        kernel,
        out_shape=out_shape,
        scratch_shapes=scratch,
        compiler_params=pltpu.CompilerParams(vmem_limit_bytes=vmem_limit),
        cost_estimate=pl.CostEstimate(flops=flops, bytes_accessed=0, transcendentals=0),
        **specs,
    )


def copy_kernel(own_ref, copies_ref, extra_ref):
    copies_ref[...] = jnp.broadcast_to(own_ref[:cells][None], copies_ref.shape)
    last = own_ref[cells:].astype(f32)
    lanes = extra_ref.shape[1]
    pieces = last.shape[1] // lanes
    for piece in range(pieces):
        extra_ref[piece : piece + 1, :] = last[:1, piece * lanes : (piece + 1) * lanes]
    extra_ref[pieces:, :] = last[8 : 8 + clips - pieces, :lanes]


def frame_index(count):
    return lax.broadcasted_iota(jnp.int32, (count, 1), 0) % frames


def shift_rows(values, step):
    count = values.shape[0]
    frame = frame_index(count)
    if step == 1:
        return jnp.where(frame == 0, 0.0, pltpu.roll(values, 1, 0))
    return jnp.where(frame == frames - 1, 0.0, pltpu.roll(values, count - 1, 0))


def forward_kernel(
    group_ref,
    weight_ref,
    projection_ref,
    extra_ref,
    slope_ref,
    turned_ref,
    partial_ref,
):
    inputs = group_ref[...].reshape(clips * cells, -1)
    turned = inputs.T.astype(f32).reshape(2, heights, 2, 2, 8, clips * cells)
    turned = jnp.concatenate([turned[:, first_far:], turned[:, :first_far]], axis=1)
    block = heights * 8
    for core in range(2):
        for yhi in range(2):
            for zl in range(2):
                rows = turned[yhi, :, zl, core].reshape(block, clips * cells)
                low = (2 * yhi + zl) * block
                turned_ref[core, low : low + block] = rows.astype(bf16)
    out_width = projection_ref.shape[0]
    preact = None
    for a in range(3):
        product = jnp.dot(
            inputs,
            jnp.concatenate([weight_ref[3 * a + b] for b in range(3)], axis=1),
            preferred_element_type=f32,
        ).reshape(clips, freq, frames, 3 * out_width)
        low = product[..., :out_width]
        mid = product[..., out_width : 2 * out_width]
        high = product[..., 2 * out_width :]
        bins = []
        for f in range(freq):
            total = mid[:, f]
            if f > 0:
                total = total + low[:, f - 1]
            if f < freq - 1:
                total = total + high[:, f + 1]
            bins.append(total[:, None])
        column = jnp.concatenate(bins, axis=1).reshape(clips * cells, out_width)
        if a == 0:
            column = shift_rows(column, 1)
        if a == 2:
            column = shift_rows(column, -1)
        preact = column if preact is None else preact + column
    sigma = jax.nn.sigmoid(preact)
    slope_ref[...] = sigma * (1.0 + preact * (1.0 - sigma))
    active = (preact * sigma).reshape(clips, cells, out_width)
    pooled = (jnp.sum(active, axis=1) * (1.0 / cells)).astype(bf16)
    partial = jnp.dot(pooled, projection_ref[...], preferred_element_type=f32)
    embed = partial.shape[1]
    partial_ref[:, :, :embed] = jnp.broadcast_to(partial[None], (clips, clips, embed))
    partial_ref[:, :, embed:] = jnp.broadcast_to(
        extra_ref[...][None], (clips, clips, extra_ref.shape[1])
    )


def row_sum(values):
    return jnp.sum(values, axis=-1, keepdims=True)


def pair_column(audio_unit, caption_row, clip_labels, column):
    logits = logit_scale * row_sum(audio_unit * caption_row) + logit_bias
    signs = jnp.where(clip_labels == column, 1.0, -1.0)
    return -loss_scale * signs * jax.nn.sigmoid(-signs * logits)


def shift_all(pre_grad, shifted_ref):
    width = pre_grad.shape[1]
    zeros = jnp.zeros((clips, frames, width), bf16)
    for a in range(3):
        moved = pre_grad
        if a == 0:
            moved = shift_rows(pre_grad, -1)
        if a == 2:
            moved = shift_rows(pre_grad, 1)
        moved = moved.astype(bf16).reshape(clips, freq, frames, width)
        for b in range(3):
            tap = 3 * a + b
            for f in range(freq):
                source = f - (b - 1)
                block = moved[:, source] if 0 <= source < freq else zeros
                shifted_ref[:, f, :, tap * width : (tap + 1) * width] = block
    return shifted_ref[...].reshape(clips * cells, -1)


def pair_kernel(
    parts_ref,
    slope_ref,
    projection_ref,
    turned_ref,
    text_ref,
    pre_ref,
    sent_ref,
    shifted_ref,
):
    core = lax.axis_index("core")
    embed = projection_ref.shape[1]
    lanes = parts_ref.shape[2] - embed
    embedding = jnp.sum(parts_ref[:, :, :embed], axis=0)
    inv_audio = lax.rsqrt(row_sum(embedding * embedding) + norm_eps)
    audio_unit = embedding * inv_audio
    clip_labels = jnp.concatenate(
        [parts_ref[c, clips - 1 :, embed : embed + 1] for c in range(clips)], axis=0
    ).astype(jnp.int32)
    position = lax.axis_index("ylo") * columns + lax.axis_index("x")

    def caption_at(index):
        text_values = jnp.concatenate(
            [parts_ref[index, p : p + 1, embed:] for p in range(embed // lanes)], axis=1
        )
        inv_text = lax.rsqrt(row_sum(text_values * text_values) + norm_eps)
        return text_values * inv_text, inv_text

    audio_grad = jnp.zeros_like(audio_unit)
    for j in range(clips):
        caption, _ = caption_at(j)
        audio_grad = audio_grad + pair_column(audio_unit, caption, clip_labels, j) * caption
    audio_grad = logit_scale * audio_grad
    caption, inv_text = caption_at(position)
    own_pairs = pair_column(audio_unit, caption, clip_labels, position)
    caption_grad = logit_scale * jnp.sum(own_pairs * audio_unit, axis=0, keepdims=True)
    text_ref[...] = (caption_grad - caption * row_sum(caption * caption_grad)) * inv_text
    embedding_grad = (
        (audio_grad - audio_unit * row_sum(audio_unit * audio_grad)) * inv_audio
    ).astype(bf16)
    pooled_grad = lax.dot_general(
        embedding_grad, projection_ref[...], (((1,), (1,)), ((), ())), preferred_element_type=f32
    )
    width = pooled_grad.shape[1]
    scaled = pooled_grad * (1.0 / cells)
    pre_grad = (scaled[:, None, :] * slope_ref[...].reshape(clips, cells, width)).astype(bf16)
    pre_grad = pre_grad.astype(f32).reshape(clips * cells, width)
    pre_ref[...] = pre_grad.astype(bf16)
    shifted = shift_all(pre_grad, shifted_ref)
    sent_ref[...] = jnp.dot(turned_ref[1 - core], shifted, preferred_element_type=f32).astype(bf16)


def keep_kernel(turned_ref, pre_ref, weight_ref, kept_ref, *rest):
    out_refs, total_ref, shifted_ref = rest[:columns], rest[columns], rest[columns + 1]
    core = lax.axis_index("core")
    shifted = shift_all(pre_ref[...].astype(f32), shifted_ref)
    kept_ref[...] = jnp.dot(turned_ref[core], shifted, preferred_element_type=f32)
    weight = jnp.concatenate([weight_ref[tap] for tap in range(weight_ref.shape[0])], axis=1)
    result = lax.dot_general(
        shifted, weight, (((1,), (1,)), ((), ())), preferred_element_type=f32
    )
    total_ref[...] = result.astype(bf16).reshape(total_ref.shape)
    here = lax.axis_index("x")
    for d in range(columns):
        out_refs[d][...] = total_ref[:, here ^ d]


def pair_sum_kernel(kept_ref, came_ref, sent_ref, sent_buf, sems):
    copies = []
    count = sent_buf.shape[1]
    for piece in range(sent_buf.shape[0]):
        rows = slice(piece * count, (piece + 1) * count)
        sent_buf[piece] = (kept_ref[rows] + came_ref[rows].astype(f32)).astype(bf16)
        copies.append(
            pltpu.make_async_copy(sent_buf.at[piece], sent_ref.at[piece], sems.at[piece])
        )
        copies[-1].start()
    for copy in copies:
        copy.wait()


def add_kernel(parts_ref, after_ref, sent_ref, sent_buf, sem):
    sent_buf[...] = jnp.sum(parts_ref[...].astype(f32), axis=0).astype(bf16)
    copy = pltpu.make_async_copy(sent_buf, sent_ref, sem)
    copy.start()
    copy.wait()


def near_kernel(own_ref, a_ref, b_ref, total_ref):
    total_ref[...] = own_ref[...].astype(f32) + a_ref[...].astype(f32) + b_ref[...].astype(f32)


def column_kernel(near_ref, c_ref, mine_ref, sent_ref, total_ref):
    total_ref[...] = near_ref[...] + c_ref[...].astype(f32)
    side = lax.axis_index("ylo")
    mine_ref[...] = total_ref[side]
    sent_ref[...] = total_ref[1 - side].astype(bf16)


def join_kernel(mine_ref, came_ref, out_ref):
    out_ref[...] = (mine_ref[...] + came_ref[...].astype(f32)).astype(bf16)


def final_kernel(group_total, parts_ref, out_ref):
    total = jnp.sum(parts_ref[...].astype(f32), axis=0) * (1.0 / group_total)
    taps, _, width = out_ref.shape
    for tap in range(taps):
        out_ref[tap] = total[:, tap * width : (tap + 1) * width]


def swap(values, axis):
    return lax.ppermute(values, axis, [(0, 1), (1, 0)])


def shards(features, conv_weight, projection, text, labels):
    taps, channels, width = conv_weight.shape
    wide = taps * width
    embed = projection.shape[1]
    half = channels // 2
    quarter = half // 4
    matmul = 2 * clips * cells * channels * wide
    own = jnp.concatenate(
        [
            features.reshape(cells, channels),
            text.reshape(1, channels),
            jnp.broadcast_to(labels.astype(bf16), (15, channels)),
        ]
    )
    copies, extra = call(
        copy_kernel, (shape((clips, cells, channels), bf16), shape((clips, 128), f32))
    )(own)
    group = lax.all_to_all(copies, BLK, 0, 0)
    slope, turned, partial = call(
        forward_kernel,
        (
            shape((clips * cells, width), f32),
            shape((2, half, clips * cells), bf16),
            shape((clips, clips, embed + 128), f32),
        ),
        flops=matmul,
    )(group, conv_weight, projection, extra)
    parts = lax.all_to_all(partial, BLK, 0, 0)
    shifted_buf = pltpu.VMEM((clips, freq, frames, wide), bf16)
    grad_text, pre, sent = call(
        pair_kernel,
        (
            shape((1, embed), f32),
            shape((clips * cells, width), bf16),
            shape((half, wide), bf16),
        ),
        scratch=[shifted_buf],
        flops=matmul // 2,
    )(parts, slope, projection, turned)
    kept, *columns_out = call(
        keep_kernel,
        (shape((half, wide), f32),)
        + tuple(shape((2, cells, channels), bf16) for _ in range(columns)),
        scratch=[pltpu.VMEM((2, columns, cells, channels), bf16), shifted_buf],
        flops=matmul + matmul // 2,
    )(turned, pre, conv_weight)
    came = swap(sent, "core")
    sent = call(
        pair_sum_kernel,
        shape((4, quarter, wide), bf16),
        scratch=[pltpu.VMEM((4, quarter, wide), bf16), DMA((4,))],
        out_specs=HBM,
    )(kept, came)
    parts = lax.all_to_all(sent, NEAR, 0, 0)
    sent = call(
        add_kernel,
        shape((quarter, wide), bf16),
        scratch=[pltpu.VMEM((quarter, wide), bf16), DMA],
        in_specs=[VMEM, pl.BlockSpec(memory_space=pl.ANY)],
        out_specs=HBM,
    )(parts, columns_out[0])
    parts = lax.all_to_all(
        sent.reshape(heights, quarter // heights, wide), FAR, 0, 0, axis_index_groups=[far_order]
    )
    others = [
        lax.ppermute(columns_out[d], "x", [(i, i ^ d) for i in range(columns)])
        for d in range(1, columns)
    ]
    near = call(near_kernel, shape((2, cells, channels), f32), flops=int(2e10))(
        columns_out[0], others[0], others[2]
    )
    mine, other = call(
        column_kernel,
        (shape((cells, channels), f32), shape((cells, channels), bf16)),
        scratch=[pltpu.VMEM((2, cells, channels), f32)],
        flops=int(3e9),
    )(near, others[1])
    grad_features = call(join_kernel, shape((cells, channels), bf16))(mine, swap(other, "ylo"))
    grad_weight = call(
        functools.partial(final_kernel, heights * 8),
        shape((taps, quarter // heights, width), f32),
    )(parts)
    return (
        grad_features.reshape(features.shape),
        grad_weight,
        grad_text.reshape(1, 1, embed),
    )


def solution(mesh):
    fine = Mesh(mesh.devices.reshape(2, columns, 2, 8, 2, 2), ("ylo", "x", "yhi", "z8", "zl", "core"))
    dp = ("yhi", "z8", "zl", "core")
    placed = (
        P(BLK, dp, None, None, None),
        P(None, None, BLK),
        P(BLK, None),
        P(BLK, dp, None),
        P(BLK, dp),
    )
    return jax.shard_map(
        shards,
        mesh=fine,
        in_specs=placed,
        out_specs=(P(BLK, dp, None, None, None), P(None, dp, BLK), P(BLK, dp, None)),
        check_vma=False,
    )
```

```python
import functools

import jax
import jax.numpy as jnp
from jax import lax
from jax.experimental import pallas as pl
from jax.experimental.pallas import tpu as pltpu
from jax.sharding import Mesh, PartitionSpec as P

logit_scale = 10.0
logit_bias = -2.0
loss_scale = 1024.0
norm_eps = 1e-06

BLK = ("ylo", "x")
NEAR = ("yhi", "zl")
FAR = "z8"
f32 = jnp.float32
bf16 = jnp.bfloat16

clips = 8
freq = 4
frames = 32
cells = freq * frames
columns = 4
heights = 8
first_far = 4
far_order = [(first_far + p) % heights for p in range(heights)]
vmem_limit = 40 * 1024 * 1024
HBM = pl.BlockSpec(memory_space=pltpu.HBM)
VMEM = pl.BlockSpec(memory_space=pltpu.VMEM)
DMA = pltpu.SemaphoreType.DMA


def shape(dims, dtype):
    return jax.ShapeDtypeStruct(dims, dtype)


def call(kernel, out_shape, scratch=(), flops=0, **specs):
    return pl.pallas_call(
        kernel,
        out_shape=out_shape,
        scratch_shapes=scratch,
        compiler_params=pltpu.CompilerParams(vmem_limit_bytes=vmem_limit),
        cost_estimate=pl.CostEstimate(flops=flops, bytes_accessed=0, transcendentals=0),
        **specs,
    )


def copy_kernel(own_ref, copies_ref, extra_ref):
    copies_ref[...] = jnp.broadcast_to(own_ref[:cells][None], copies_ref.shape)
    last = own_ref[cells:].astype(f32)
    lanes = extra_ref.shape[1]
    pieces = last.shape[1] // lanes
    for piece in range(pieces):
        extra_ref[piece : piece + 1, :] = last[:1, piece * lanes : (piece + 1) * lanes]
    extra_ref[pieces:, :] = last[8 : 8 + clips - pieces, :lanes]


def frame_index(count):
    return lax.broadcasted_iota(jnp.int32, (count, 1), 0) % frames


def shift_rows(values, step):
    count = values.shape[0]
    frame = frame_index(count)
    if step == 1:
        return jnp.where(frame == 0, 0.0, pltpu.roll(values, 1, 0))
    return jnp.where(frame == frames - 1, 0.0, pltpu.roll(values, count - 1, 0))


def forward_kernel(
    group_ref,
    weight_ref,
    projection_ref,
    extra_ref,
    slope_ref,
    turned_ref,
    partial_ref,
):
    inputs = group_ref[...].reshape(clips * cells, -1)
    turned = inputs.T.astype(f32).reshape(2, heights, 2, 2, 8, clips * cells)
    turned = jnp.concatenate([turned[:, first_far:], turned[:, :first_far]], axis=1)
    block = heights * 8
    for core in range(2):
        for yhi in range(2):
            for zl in range(2):
                rows = turned[yhi, :, zl, core].reshape(block, clips * cells)
                low = (2 * yhi + zl) * block
                turned_ref[core, low : low + block] = rows.astype(bf16)
    out_width = projection_ref.shape[0]
    weight = jnp.concatenate([weight_ref[tap] for tap in range(weight_ref.shape[0])], axis=1)
    products = jnp.dot(inputs, weight, preferred_element_type=f32)
    preact = None
    for a in range(3):
        product = products[:, 3 * a * out_width : 3 * (a + 1) * out_width].reshape(
            clips, freq, frames, 3 * out_width
        )
        low = product[..., :out_width]
        mid = product[..., out_width : 2 * out_width]
        high = product[..., 2 * out_width :]
        bins = []
        for f in range(freq):
            total = mid[:, f]
            if f > 0:
                total = total + low[:, f - 1]
            if f < freq - 1:
                total = total + high[:, f + 1]
            bins.append(total[:, None])
        column = jnp.concatenate(bins, axis=1).reshape(clips * cells, out_width)
        if a == 0:
            column = shift_rows(column, 1)
        if a == 2:
            column = shift_rows(column, -1)
        preact = column if preact is None else preact + column
    sigma = jax.nn.sigmoid(preact)
    slope_ref[...] = sigma * (1.0 + preact * (1.0 - sigma))
    active = (preact * sigma).reshape(clips, cells, out_width)
    pooled = (jnp.sum(active, axis=1) * (1.0 / cells)).astype(bf16)
    partial = jnp.dot(pooled, projection_ref[...], preferred_element_type=f32)
    embed = partial.shape[1]
    partial_ref[:, :, :embed] = jnp.broadcast_to(partial[None], (clips, clips, embed))
    partial_ref[:, :, embed:] = jnp.broadcast_to(
        extra_ref[...][None], (clips, clips, extra_ref.shape[1])
    )


def row_sum(values):
    return jnp.sum(values, axis=-1, keepdims=True)


def pair_column(audio_unit, caption_row, clip_labels, column):
    logits = logit_scale * row_sum(audio_unit * caption_row) + logit_bias
    signs = jnp.where(clip_labels == column, 1.0, -1.0)
    return -loss_scale * signs * jax.nn.sigmoid(-signs * logits)


def shift_all(pre_grad, shifted_ref):
    width = pre_grad.shape[1]
    zeros = jnp.zeros((clips, frames, width), bf16)
    for a in range(3):
        moved = pre_grad
        if a == 0:
            moved = shift_rows(pre_grad, -1)
        if a == 2:
            moved = shift_rows(pre_grad, 1)
        moved = moved.astype(bf16).reshape(clips, freq, frames, width)
        for b in range(3):
            tap = 3 * a + b
            for f in range(freq):
                source = f - (b - 1)
                block = moved[:, source] if 0 <= source < freq else zeros
                shifted_ref[:, f, :, tap * width : (tap + 1) * width] = block
    return shifted_ref[...].reshape(clips * cells, -1)


def pair_kernel(
    parts_ref,
    slope_ref,
    projection_ref,
    turned_ref,
    text_ref,
    pre_ref,
    sent_ref,
    shifted_ref,
):
    core = lax.axis_index("core")
    embed = projection_ref.shape[1]
    lanes = parts_ref.shape[2] - embed
    embedding = jnp.sum(parts_ref[:, :, :embed], axis=0)
    inv_audio = lax.rsqrt(row_sum(embedding * embedding) + norm_eps)
    audio_unit = embedding * inv_audio
    clip_labels = jnp.concatenate(
        [parts_ref[c, clips - 1 :, embed : embed + 1] for c in range(clips)], axis=0
    ).astype(jnp.int32)
    position = lax.axis_index("ylo") * columns + lax.axis_index("x")

    def caption_at(index):
        text_values = jnp.concatenate(
            [parts_ref[index, p : p + 1, embed:] for p in range(embed // lanes)], axis=1
        )
        inv_text = lax.rsqrt(row_sum(text_values * text_values) + norm_eps)
        return text_values * inv_text, inv_text

    audio_grad = jnp.zeros_like(audio_unit)
    for j in range(clips):
        caption, _ = caption_at(j)
        audio_grad = audio_grad + pair_column(audio_unit, caption, clip_labels, j) * caption
    audio_grad = logit_scale * audio_grad
    caption, inv_text = caption_at(position)
    own_pairs = pair_column(audio_unit, caption, clip_labels, position)
    caption_grad = logit_scale * jnp.sum(own_pairs * audio_unit, axis=0, keepdims=True)
    text_ref[...] = (caption_grad - caption * row_sum(caption * caption_grad)) * inv_text
    embedding_grad = (
        (audio_grad - audio_unit * row_sum(audio_unit * audio_grad)) * inv_audio
    ).astype(bf16)
    pooled_grad = lax.dot_general(
        embedding_grad, projection_ref[...], (((1,), (1,)), ((), ())), preferred_element_type=f32
    )
    width = pooled_grad.shape[1]
    scaled = pooled_grad * (1.0 / cells)
    pre_grad = (scaled[:, None, :] * slope_ref[...].reshape(clips, cells, width)).astype(bf16)
    pre_grad = pre_grad.astype(f32).reshape(clips * cells, width)
    pre_ref[...] = pre_grad.astype(bf16)
    shifted = shift_all(pre_grad, shifted_ref)
    sent_ref[...] = jnp.dot(turned_ref[1 - core], shifted, preferred_element_type=f32).astype(bf16)


def keep_kernel(turned_ref, pre_ref, weight_ref, kept_ref, *rest):
    out_refs, total_ref, shifted_ref = rest[:columns], rest[columns], rest[columns + 1]
    core = lax.axis_index("core")
    shifted = shift_all(pre_ref[...].astype(f32), shifted_ref)
    kept_ref[...] = jnp.dot(turned_ref[core], shifted, preferred_element_type=f32)
    weight = jnp.concatenate([weight_ref[tap] for tap in range(weight_ref.shape[0])], axis=1)
    result = lax.dot_general(
        shifted, weight, (((1,), (1,)), ((), ())), preferred_element_type=f32
    )
    total_ref[...] = result.astype(bf16).reshape(total_ref.shape)
    here = lax.axis_index("x")
    for d in range(columns):
        out_refs[d][...] = total_ref[:, here ^ d]


def pair_sum_kernel(kept_ref, came_ref, sent_ref, sent_buf, sems):
    copies = []
    count = sent_buf.shape[1]
    for piece in range(sent_buf.shape[0]):
        rows = slice(piece * count, (piece + 1) * count)
        sent_buf[piece] = (kept_ref[rows] + came_ref[rows].astype(f32)).astype(bf16)
        copies.append(
            pltpu.make_async_copy(sent_buf.at[piece], sent_ref.at[piece], sems.at[piece])
        )
        copies[-1].start()
    for copy in copies:
        copy.wait()


def add_kernel(parts_ref, after_ref, sent_ref, sent_buf, sem):
    sent_buf[...] = jnp.sum(parts_ref[...].astype(f32), axis=0).astype(bf16)
    copy = pltpu.make_async_copy(sent_buf, sent_ref, sem)
    copy.start()
    copy.wait()


def near_kernel(own_ref, a_ref, b_ref, total_ref):
    total_ref[...] = own_ref[...].astype(f32) + a_ref[...].astype(f32) + b_ref[...].astype(f32)


def column_kernel(near_ref, c_ref, mine_ref, sent_ref, total_ref):
    total_ref[...] = near_ref[...] + c_ref[...].astype(f32)
    side = lax.axis_index("ylo")
    mine_ref[...] = total_ref[side]
    sent_ref[...] = total_ref[1 - side].astype(bf16)


def final_kernel(group_total, parts_ref, mine_ref, came_ref, weight_out_ref, feature_out_ref):
    feature_out_ref[...] = (mine_ref[...] + came_ref[...].astype(f32)).astype(bf16)
    total = jnp.sum(parts_ref[...].astype(f32), axis=0) * (1.0 / group_total)
    taps, _, width = weight_out_ref.shape
    for tap in range(taps):
        weight_out_ref[tap] = total[:, tap * width : (tap + 1) * width]


def swap(values, axis):
    return lax.ppermute(values, axis, [(0, 1), (1, 0)])


def shards(features, conv_weight, projection, text, labels):
    taps, channels, width = conv_weight.shape
    wide = taps * width
    embed = projection.shape[1]
    half = channels // 2
    quarter = half // 4
    matmul = 2 * clips * cells * channels * wide
    own = jnp.concatenate(
        [
            features.reshape(cells, channels),
            text.reshape(1, channels),
            jnp.broadcast_to(labels.astype(bf16), (15, channels)),
        ]
    )
    copies, extra = call(
        copy_kernel, (shape((clips, cells, channels), bf16), shape((clips, 128), f32))
    )(own)
    group = lax.all_to_all(copies, BLK, 0, 0)
    slope, turned, partial = call(
        forward_kernel,
        (
            shape((clips * cells, width), f32),
            shape((2, half, clips * cells), bf16),
            shape((clips, clips, embed + 128), f32),
        ),
        flops=matmul,
    )(group, conv_weight, projection, extra)
    parts = lax.all_to_all(partial, BLK, 0, 0)
    shifted_buf = pltpu.VMEM((clips, freq, frames, wide), bf16)
    grad_text, pre, sent = call(
        pair_kernel,
        (
            shape((1, embed), f32),
            shape((clips * cells, width), bf16),
            shape((half, wide), bf16),
        ),
        scratch=[shifted_buf],
        flops=matmul // 2,
    )(parts, slope, projection, turned)
    kept, *columns_out = call(
        keep_kernel,
        (shape((half, wide), f32),)
        + tuple(shape((2, cells, channels), bf16) for _ in range(columns)),
        scratch=[pltpu.VMEM((2, columns, cells, channels), bf16), shifted_buf],
        flops=matmul + matmul // 2,
    )(turned, pre, conv_weight)
    came = swap(sent, "core")
    sent = call(
        pair_sum_kernel,
        shape((4, quarter, wide), bf16),
        scratch=[pltpu.VMEM((4, quarter, wide), bf16), DMA((4,))],
        out_specs=HBM,
    )(kept, came)
    parts = lax.all_to_all(sent, NEAR, 0, 0)
    sent = call(
        add_kernel,
        shape((quarter, wide), bf16),
        scratch=[pltpu.VMEM((quarter, wide), bf16), DMA],
        in_specs=[VMEM, pl.BlockSpec(memory_space=pl.ANY)],
        out_specs=HBM,
    )(parts, columns_out[0])
    parts = lax.all_to_all(
        sent.reshape(heights, quarter // heights, wide), FAR, 0, 0, axis_index_groups=[far_order]
    )
    others = [
        lax.ppermute(columns_out[d], "x", [(i, i ^ d) for i in range(columns)])
        for d in range(1, columns)
    ]
    near = call(near_kernel, shape((2, cells, channels), f32), flops=int(2e10))(
        columns_out[0], others[0], others[2]
    )
    mine, other = call(
        column_kernel,
        (shape((cells, channels), f32), shape((cells, channels), bf16)),
        scratch=[pltpu.VMEM((2, cells, channels), f32)],
        flops=int(3e9),
    )(near, others[1])
    grad_weight, grad_features = call(
        functools.partial(final_kernel, 64),
        (shape((taps, 8, width), f32), shape((cells, channels), bf16)),
    )(parts, mine, swap(other, "ylo"))
    return (
        grad_features.reshape(features.shape),
        grad_weight,
        grad_text.reshape(1, 1, embed),
    )


def solution(mesh):
    fine = Mesh(mesh.devices.reshape(2, columns, 2, 8, 2, 2), ("ylo", "x", "yhi", "z8", "zl", "core"))
    dp = ("yhi", "z8", "zl", "core")
    placed = (
        P(BLK, dp, None, None, None),
        P(None, None, BLK),
        P(BLK, None),
        P(BLK, dp, None),
        P(BLK, dp),
    )
    return jax.shard_map(
        shards,
        mesh=fine,
        in_specs=placed,
        out_specs=(P(BLK, dp, None, None, None), P(None, dp, BLK), P(BLK, dp, None)),
        check_vma=False,
    )
```

```python
import functools

import jax
import jax.numpy as jnp
from jax import lax
from jax.experimental import pallas as pl
from jax.experimental.pallas import tpu as pltpu
from jax.sharding import Mesh, PartitionSpec as P

logit_scale = 10.0
logit_bias = -2.0
loss_scale = 1024.0
norm_eps = 1e-06

BLK = "blk"
NEAR = ("yhi", "zl")
FAR = "z8"
f32 = jnp.float32
bf16 = jnp.bfloat16

clips = 8
freq = 4
frames = 32
cells = freq * frames
columns = 4
last_member = clips - 1
blk_order = [last_member - p for p in range(clips)]
heights = 8
far_order = [5, 4, 3, 6, 2, 7, 1, 0]
vmem_limit = 40 * 1024 * 1024
HBM = pl.BlockSpec(memory_space=pltpu.HBM)
VMEM = pl.BlockSpec(memory_space=pltpu.VMEM)
DMA = pltpu.SemaphoreType.DMA


def shape(dims, dtype):
    return jax.ShapeDtypeStruct(dims, dtype)


def call(kernel, out_shape, scratch=(), flops=0, **specs):
    return pl.pallas_call(
        kernel,
        out_shape=out_shape,
        scratch_shapes=scratch,
        compiler_params=pltpu.CompilerParams(vmem_limit_bytes=vmem_limit),
        cost_estimate=pl.CostEstimate(flops=flops, bytes_accessed=0, transcendentals=0),
        **specs,
    )


def copy_kernel(own_ref, copies_ref, extra_ref):
    copies_ref[...] = jnp.broadcast_to(own_ref[:cells][None], copies_ref.shape)
    last = own_ref[cells:].astype(f32)
    lanes = extra_ref.shape[1]
    pieces = last.shape[1] // lanes
    for piece in range(pieces):
        extra_ref[piece : piece + 1, :] = last[:1, piece * lanes : (piece + 1) * lanes]
    extra_ref[pieces:, :] = last[8 : 8 + clips - pieces, :lanes]


def frame_index(count):
    return lax.broadcasted_iota(jnp.int32, (count, 1), 0) % frames


def shift_rows(values, step):
    count = values.shape[0]
    frame = frame_index(count)
    if step == 1:
        return jnp.where(frame == 0, 0.0, pltpu.roll(values, 1, 0))
    return jnp.where(frame == frames - 1, 0.0, pltpu.roll(values, count - 1, 0))


def forward_kernel(
    group_ref,
    weight_ref,
    projection_ref,
    extra_ref,
    slope_ref,
    turned_ref,
    partial_ref,
):
    inputs = group_ref[...].reshape(clips * cells, -1)
    turned = inputs.T.astype(f32).reshape(2, heights, 2, 2, 8, clips * cells)
    turned = jnp.concatenate([turned[:, z : z + 1] for z in far_order], axis=1)
    block = heights * 8
    for core in range(2):
        for yhi in range(2):
            for zl in range(2):
                rows = turned[yhi, :, zl, core].reshape(block, clips * cells)
                low = (2 * yhi + zl) * block
                turned_ref[core, low : low + block] = rows.astype(bf16)
    out_width = projection_ref.shape[0]
    weight = jnp.concatenate([weight_ref[tap] for tap in range(weight_ref.shape[0])], axis=1)
    products = jnp.dot(inputs, weight, preferred_element_type=f32)
    preact = None
    for a in range(3):
        product = products[:, 3 * a * out_width : 3 * (a + 1) * out_width].reshape(
            clips, freq, frames, 3 * out_width
        )
        low = product[..., :out_width]
        mid = product[..., out_width : 2 * out_width]
        high = product[..., 2 * out_width :]
        bins = []
        for f in range(freq):
            total = mid[:, f]
            if f > 0:
                total = total + low[:, f - 1]
            if f < freq - 1:
                total = total + high[:, f + 1]
            bins.append(total[:, None])
        column = jnp.concatenate(bins, axis=1).reshape(clips * cells, out_width)
        if a == 0:
            column = shift_rows(column, 1)
        if a == 2:
            column = shift_rows(column, -1)
        preact = column if preact is None else preact + column
    sigma = jax.nn.sigmoid(preact)
    slope_ref[...] = sigma * (1.0 + preact * (1.0 - sigma))
    active = (preact * sigma).reshape(clips, cells, out_width)
    pooled = (jnp.sum(active, axis=1) * (1.0 / cells)).astype(bf16)
    partial = jnp.dot(pooled, projection_ref[...], preferred_element_type=f32)
    embed = partial.shape[1]
    partial_ref[:, :, :embed] = jnp.broadcast_to(partial[None], (clips, clips, embed))
    partial_ref[:, :, embed:] = jnp.broadcast_to(
        extra_ref[...][None], (clips, clips, extra_ref.shape[1])
    )


def row_sum(values):
    return jnp.sum(values, axis=-1, keepdims=True)


def pair_column(audio_unit, caption_row, clip_labels, column):
    logits = logit_scale * row_sum(audio_unit * caption_row) + logit_bias
    signs = jnp.where(clip_labels == column, 1.0, -1.0)
    return -loss_scale * signs * jax.nn.sigmoid(-signs * logits)


def shift_all(pre_grad, shifted_ref):
    width = pre_grad.shape[1]
    zeros = jnp.zeros((clips, frames, width), bf16)
    for a in range(3):
        moved = pre_grad
        if a == 0:
            moved = shift_rows(pre_grad, -1)
        if a == 2:
            moved = shift_rows(pre_grad, 1)
        moved = moved.astype(bf16).reshape(clips, freq, frames, width)
        for b in range(3):
            tap = 3 * a + b
            for f in range(freq):
                source = f - (b - 1)
                block = moved[:, source] if 0 <= source < freq else zeros
                shifted_ref[:, f, :, tap * width : (tap + 1) * width] = block
    return shifted_ref[...].reshape(clips * cells, -1)


def pair_kernel(
    parts_ref,
    slope_ref,
    projection_ref,
    turned_ref,
    text_ref,
    pre_ref,
    sent_ref,
    shifted_ref,
):
    core = lax.axis_index("core")
    embed = projection_ref.shape[1]
    lanes = parts_ref.shape[2] - embed
    embedding = jnp.sum(parts_ref[:, :, :embed], axis=0)
    inv_audio = lax.rsqrt(row_sum(embedding * embedding) + norm_eps)
    audio_unit = embedding * inv_audio
    clip_labels = jnp.concatenate(
        [parts_ref[c, clips - 1 :, embed : embed + 1] for c in range(clips)], axis=0
    ).astype(jnp.int32)
    member = lax.axis_index(BLK)
    place = last_member - member

    def caption_at(index):
        text_values = jnp.concatenate(
            [parts_ref[index, p : p + 1, embed:] for p in range(embed // lanes)], axis=1
        )
        inv_text = lax.rsqrt(row_sum(text_values * text_values) + norm_eps)
        return text_values * inv_text, inv_text

    audio_grad = jnp.zeros_like(audio_unit)
    for j in range(clips):
        caption, _ = caption_at(j)
        audio_grad = (
            audio_grad + pair_column(audio_unit, caption, clip_labels, last_member - j) * caption
        )
    audio_grad = logit_scale * audio_grad
    caption, inv_text = caption_at(place)
    own_pairs = pair_column(audio_unit, caption, clip_labels, member)
    caption_grad = logit_scale * jnp.sum(own_pairs * audio_unit, axis=0, keepdims=True)
    text_ref[...] = (caption_grad - caption * row_sum(caption * caption_grad)) * inv_text
    embedding_grad = (
        (audio_grad - audio_unit * row_sum(audio_unit * audio_grad)) * inv_audio
    ).astype(bf16)
    pooled_grad = lax.dot_general(
        embedding_grad, projection_ref[...], (((1,), (1,)), ((), ())), preferred_element_type=f32
    )
    width = pooled_grad.shape[1]
    scaled = pooled_grad * (1.0 / cells)
    pre_grad = (scaled[:, None, :] * slope_ref[...].reshape(clips, cells, width)).astype(bf16)
    pre_grad = pre_grad.astype(f32).reshape(clips * cells, width)
    pre_ref[...] = pre_grad.astype(bf16)
    shifted = shift_all(pre_grad, shifted_ref)
    sent_ref[...] = jnp.dot(turned_ref[1 - core], shifted, preferred_element_type=f32).astype(bf16)


def keep_kernel(turned_ref, pre_ref, weight_ref, kept_ref, *rest):
    out_refs, total_ref, shifted_ref = rest[:columns], rest[columns], rest[columns + 1]
    core = lax.axis_index("core")
    shifted = shift_all(pre_ref[...].astype(f32), shifted_ref)
    kept_ref[...] = jnp.dot(turned_ref[core], shifted, preferred_element_type=f32)
    weight = jnp.concatenate([weight_ref[tap] for tap in range(weight_ref.shape[0])], axis=1)
    result = lax.dot_general(
        shifted, weight, (((1,), (1,)), ((), ())), preferred_element_type=f32
    )
    total_ref[...] = result.astype(bf16).reshape(total_ref.shape)
    here = lax.axis_index(BLK) % columns
    for d in range(columns):
        out_refs[d][...] = total_ref[:, (columns - 1 - here) ^ d]


def pair_sum_kernel(kept_ref, came_ref, sent_ref, sent_buf, sems):
    copies = []
    count = sent_buf.shape[1]
    for piece in range(sent_buf.shape[0]):
        rows = slice(piece * count, (piece + 1) * count)
        sent_buf[piece] = (kept_ref[rows] + came_ref[rows].astype(f32)).astype(bf16)
        copies.append(
            pltpu.make_async_copy(sent_buf.at[piece], sent_ref.at[piece], sems.at[piece])
        )
        copies[-1].start()
    for copy in copies:
        copy.wait()


def add_kernel(parts_ref, after_ref, sent_ref, sent_buf, sem):
    sent_buf[...] = jnp.sum(parts_ref[...].astype(f32), axis=0).astype(bf16)
    copy = pltpu.make_async_copy(sent_buf, sent_ref, sem)
    copy.start()
    copy.wait()


def near_kernel(own_ref, a_ref, b_ref, total_ref):
    total_ref[...] = own_ref[...].astype(f32) + a_ref[...].astype(f32) + b_ref[...].astype(f32)


def column_kernel(near_ref, c_ref, mine_ref, sent_ref, total_ref):
    total_ref[...] = near_ref[...] + c_ref[...].astype(f32)
    side = 1 - lax.axis_index(BLK) // columns
    mine_ref[...] = total_ref[side]
    sent_ref[...] = total_ref[1 - side].astype(bf16)


def final_kernel(group_total, parts_ref, mine_ref, came_ref, weight_out_ref, feature_out_ref):
    feature_out_ref[...] = (mine_ref[...] + came_ref[...].astype(f32)).astype(bf16)
    total = jnp.sum(parts_ref[...].astype(f32), axis=0) * (1.0 / group_total)
    taps, _, width = weight_out_ref.shape
    for tap in range(taps):
        weight_out_ref[tap] = total[:, tap * width : (tap + 1) * width]


def swap(values, axis):
    return lax.ppermute(values, axis, [(0, 1), (1, 0)])


def shards(features, conv_weight, projection, text, labels):
    taps, channels, width = conv_weight.shape
    wide = taps * width
    embed = projection.shape[1]
    half = channels // 2
    quarter = half // 4
    matmul = 2 * clips * cells * channels * wide
    own = jnp.concatenate(
        [
            features.reshape(cells, channels),
            text.reshape(1, channels),
            jnp.broadcast_to(labels.astype(bf16), (15, channels)),
        ]
    )
    copies, extra = call(
        copy_kernel, (shape((clips, cells, channels), bf16), shape((clips, 128), f32))
    )(own)
    group = lax.all_to_all(copies, BLK, 0, 0, axis_index_groups=[blk_order])
    slope, turned, partial = call(
        forward_kernel,
        (
            shape((clips * cells, width), f32),
            shape((2, half, clips * cells), bf16),
            shape((clips, clips, embed + 128), f32),
        ),
        flops=matmul,
    )(group, conv_weight, projection, extra)
    parts = lax.all_to_all(partial, BLK, 0, 0, axis_index_groups=[blk_order])
    shifted_buf = pltpu.VMEM((clips, freq, frames, wide), bf16)
    grad_text, pre, sent = call(
        pair_kernel,
        (
            shape((1, embed), f32),
            shape((clips * cells, width), bf16),
            shape((half, wide), bf16),
        ),
        scratch=[shifted_buf],
        flops=matmul // 2,
    )(parts, slope, projection, turned)
    kept, *columns_out = call(
        keep_kernel,
        (shape((half, wide), f32),)
        + tuple(shape((2, cells, channels), bf16) for _ in range(columns)),
        scratch=[pltpu.VMEM((2, columns, cells, channels), bf16), shifted_buf],
        flops=matmul + matmul // 2,
    )(turned, pre, conv_weight)
    came = swap(sent, "core")
    sent = call(
        pair_sum_kernel,
        shape((4, quarter, wide), bf16),
        scratch=[pltpu.VMEM((4, quarter, wide), bf16), DMA((4,))],
        out_specs=HBM,
    )(kept, came)
    parts = lax.all_to_all(sent, NEAR, 0, 0)
    sent = call(
        add_kernel,
        shape((quarter, wide), bf16),
        scratch=[pltpu.VMEM((quarter, wide), bf16), DMA],
        in_specs=[VMEM, pl.BlockSpec(memory_space=pl.ANY)],
        out_specs=HBM,
    )(parts, columns_out[0])
    parts = lax.all_to_all(
        sent.reshape(heights, quarter // heights, wide), FAR, 0, 0, axis_index_groups=[far_order]
    )
    others = [
        lax.ppermute(columns_out[d], BLK, [(i, i ^ d) for i in range(clips)])
        for d in range(1, columns)
    ]
    near = call(near_kernel, shape((2, cells, channels), f32), flops=int(2e10))(
        columns_out[0], others[0], others[2]
    )
    mine, other = call(
        column_kernel,
        (shape((cells, channels), f32), shape((cells, channels), bf16)),
        scratch=[pltpu.VMEM((2, cells, channels), f32)],
        flops=int(3e9),
    )(near, others[1])
    grad_weight, grad_features = call(
        functools.partial(final_kernel, 64),
        (shape((taps, 8, width), f32), shape((cells, channels), bf16)),
    )(parts, mine, lax.ppermute(other, BLK, [(i, i ^ columns) for i in range(clips)]))
    return (
        grad_features.reshape(features.shape),
        grad_weight,
        grad_text.reshape(1, 1, embed),
    )


def solution(mesh):
    fine = Mesh(mesh.devices.reshape(clips, 2, 8, 2, 2), ("blk", "yhi", "z8", "zl", "core"))
    dp = ("yhi", "z8", "zl", "core")
    placed = (
        P(BLK, dp, None, None, None),
        P(None, None, BLK),
        P(BLK, None),
        P(BLK, dp, None),
        P(BLK, dp),
    )
    return jax.shard_map(
        shards,
        mesh=fine,
        in_specs=placed,
        out_specs=(P(BLK, dp, None, None, None), P(None, dp, BLK), P(BLK, dp, None)),
        check_vma=False,
    )
```

```python
import functools

import jax
import jax.numpy as jnp
from jax import lax
from jax.experimental import pallas as pl
from jax.experimental.pallas import tpu as pltpu
from jax.sharding import Mesh, PartitionSpec as P

logit_scale = 10.0
logit_bias = -2.0
loss_scale = 1024.0
norm_eps = 1e-06

BLK = "blk"
NEAR = ("yhi", "zl")
FAR = "z8"
f32 = jnp.float32
bf16 = jnp.bfloat16

clips = 8
freq = 4
frames = 32
cells = freq * frames
columns = 4
last_member = clips - 1
blk_order = [last_member - p for p in range(clips)]
heights = 8
far_order = [5, 4, 3, 2, 1, 0, 7, 6]
vmem_limit = 40 * 1024 * 1024
HBM = pl.BlockSpec(memory_space=pltpu.HBM)
VMEM = pl.BlockSpec(memory_space=pltpu.VMEM)
DMA = pltpu.SemaphoreType.DMA


def shape(dims, dtype):
    return jax.ShapeDtypeStruct(dims, dtype)


def call(kernel, out_shape, scratch=(), flops=0, **specs):
    return pl.pallas_call(
        kernel,
        out_shape=out_shape,
        scratch_shapes=scratch,
        compiler_params=pltpu.CompilerParams(vmem_limit_bytes=vmem_limit),
        cost_estimate=pl.CostEstimate(flops=flops, bytes_accessed=0, transcendentals=0),
        **specs,
    )


def copy_kernel(own_ref, copies_ref, extra_ref):
    copies_ref[...] = jnp.broadcast_to(own_ref[:cells][None], copies_ref.shape)
    last = own_ref[cells:].astype(f32)
    lanes = extra_ref.shape[1]
    pieces = last.shape[1] // lanes
    for piece in range(pieces):
        extra_ref[piece : piece + 1, :] = last[:1, piece * lanes : (piece + 1) * lanes]
    extra_ref[pieces:, :] = last[8 : 8 + clips - pieces, :lanes]


def frame_index(count):
    return lax.broadcasted_iota(jnp.int32, (count, 1), 0) % frames


def shift_rows(values, step):
    count = values.shape[0]
    frame = frame_index(count)
    if step == 1:
        return jnp.where(frame == 0, 0.0, pltpu.roll(values, 1, 0))
    return jnp.where(frame == frames - 1, 0.0, pltpu.roll(values, count - 1, 0))


def forward_kernel(
    group_ref,
    weight_ref,
    projection_ref,
    extra_ref,
    slope_ref,
    turned_ref,
    partial_ref,
):
    inputs = group_ref[...].reshape(clips * cells, -1)
    turned = inputs.T.astype(f32).reshape(2, heights, 2, 2, 8, clips * cells)
    turned = jnp.concatenate([turned[:, z : z + 1] for z in far_order], axis=1)
    block = heights * 8
    for core in range(2):
        for yhi in range(2):
            for zl in range(2):
                rows = turned[yhi, :, zl, core].reshape(block, clips * cells)
                low = (2 * yhi + zl) * block
                turned_ref[core, low : low + block] = rows.astype(bf16)
    out_width = projection_ref.shape[0]
    weight = jnp.concatenate([weight_ref[tap] for tap in range(weight_ref.shape[0])], axis=1)
    products = jnp.dot(inputs, weight, preferred_element_type=f32)
    preact = None
    for a in range(3):
        product = products[:, 3 * a * out_width : 3 * (a + 1) * out_width].reshape(
            clips, freq, frames, 3 * out_width
        )
        low = product[..., :out_width]
        mid = product[..., out_width : 2 * out_width]
        high = product[..., 2 * out_width :]
        bins = []
        for f in range(freq):
            total = mid[:, f]
            if f > 0:
                total = total + low[:, f - 1]
            if f < freq - 1:
                total = total + high[:, f + 1]
            bins.append(total[:, None])
        column = jnp.concatenate(bins, axis=1).reshape(clips * cells, out_width)
        if a == 0:
            column = shift_rows(column, 1)
        if a == 2:
            column = shift_rows(column, -1)
        preact = column if preact is None else preact + column
    sigma = jax.nn.sigmoid(preact)
    slope_ref[...] = sigma * (1.0 + preact * (1.0 - sigma))
    active = (preact * sigma).reshape(clips, cells, out_width)
    pooled = (jnp.sum(active, axis=1) * (1.0 / cells)).astype(bf16)
    partial = jnp.dot(pooled, projection_ref[...], preferred_element_type=f32)
    embed = partial.shape[1]
    partial_ref[:, :, :embed] = jnp.broadcast_to(partial[None], (clips, clips, embed))
    partial_ref[:, :, embed:] = jnp.broadcast_to(
        extra_ref[...][None], (clips, clips, extra_ref.shape[1])
    )


def row_sum(values):
    return jnp.sum(values, axis=-1, keepdims=True)


def pair_column(audio_unit, caption_row, clip_labels, column):
    logits = logit_scale * row_sum(audio_unit * caption_row) + logit_bias
    signs = jnp.where(clip_labels == column, 1.0, -1.0)
    return -loss_scale * signs * jax.nn.sigmoid(-signs * logits)


def shift_all(pre_grad, shifted_ref):
    width = pre_grad.shape[1]
    zeros = jnp.zeros((clips, frames, width), bf16)
    for a in range(3):
        moved = pre_grad
        if a == 0:
            moved = shift_rows(pre_grad, -1)
        if a == 2:
            moved = shift_rows(pre_grad, 1)
        moved = moved.astype(bf16).reshape(clips, freq, frames, width)
        for b in range(3):
            tap = 3 * a + b
            for f in range(freq):
                source = f - (b - 1)
                block = moved[:, source] if 0 <= source < freq else zeros
                shifted_ref[:, f, :, tap * width : (tap + 1) * width] = block
    return shifted_ref[...].reshape(clips * cells, -1)


def pair_kernel(
    parts_ref,
    slope_ref,
    projection_ref,
    turned_ref,
    text_ref,
    shifted_ref,
    sent_ref,
):
    core = lax.axis_index("core")
    embed = projection_ref.shape[1]
    lanes = parts_ref.shape[2] - embed
    embedding = jnp.sum(parts_ref[:, :, :embed], axis=0)
    inv_audio = lax.rsqrt(row_sum(embedding * embedding) + norm_eps)
    audio_unit = embedding * inv_audio
    clip_labels = jnp.concatenate(
        [parts_ref[c, clips - 1 :, embed : embed + 1] for c in range(clips)], axis=0
    ).astype(jnp.int32)
    member = lax.axis_index(BLK)
    place = last_member - member

    def caption_at(index):
        text_values = jnp.concatenate(
            [parts_ref[index, p : p + 1, embed:] for p in range(embed // lanes)], axis=1
        )
        inv_text = lax.rsqrt(row_sum(text_values * text_values) + norm_eps)
        return text_values * inv_text, inv_text

    audio_grad = jnp.zeros_like(audio_unit)
    for j in range(clips):
        caption, _ = caption_at(j)
        audio_grad = (
            audio_grad + pair_column(audio_unit, caption, clip_labels, last_member - j) * caption
        )
    audio_grad = logit_scale * audio_grad
    caption, inv_text = caption_at(place)
    own_pairs = pair_column(audio_unit, caption, clip_labels, member)
    caption_grad = logit_scale * jnp.sum(own_pairs * audio_unit, axis=0, keepdims=True)
    text_ref[...] = (caption_grad - caption * row_sum(caption * caption_grad)) * inv_text
    embedding_grad = (
        (audio_grad - audio_unit * row_sum(audio_unit * audio_grad)) * inv_audio
    ).astype(bf16)
    pooled_grad = lax.dot_general(
        embedding_grad, projection_ref[...], (((1,), (1,)), ((), ())), preferred_element_type=f32
    )
    width = pooled_grad.shape[1]
    scaled = pooled_grad * (1.0 / cells)
    pre_grad = (scaled[:, None, :] * slope_ref[...].reshape(clips, cells, width)).astype(bf16)
    pre_grad = pre_grad.astype(f32).reshape(clips * cells, width)
    shifted = shift_all(pre_grad, shifted_ref)
    sent_ref[...] = jnp.dot(turned_ref[1 - core], shifted, preferred_element_type=f32).astype(bf16)


def keep_kernel(turned_ref, shifted_ref, weight_ref, kept_ref, *rest):
    out_refs, total_ref = rest[:columns], rest[columns]
    core = lax.axis_index("core")
    shifted = shifted_ref[...].reshape(clips * cells, -1)
    kept_ref[...] = jnp.dot(turned_ref[core], shifted, preferred_element_type=f32)
    weight = jnp.concatenate([weight_ref[tap] for tap in range(weight_ref.shape[0])], axis=1)
    result = lax.dot_general(
        shifted, weight, (((1,), (1,)), ((), ())), preferred_element_type=f32
    )
    total_ref[...] = result.astype(bf16).reshape(total_ref.shape)
    here = lax.axis_index(BLK) % columns
    for d in range(columns):
        out_refs[d][...] = total_ref[:, (columns - 1 - here) ^ d]


def pair_sum_kernel(kept_ref, came_ref, sent_ref, sent_buf, sems):
    copies = []
    count = sent_buf.shape[1]
    for piece in range(sent_buf.shape[0]):
        rows = slice(piece * count, (piece + 1) * count)
        sent_buf[piece] = (kept_ref[rows] + came_ref[rows].astype(f32)).astype(bf16)
        copies.append(
            pltpu.make_async_copy(sent_buf.at[piece], sent_ref.at[piece], sems.at[piece])
        )
        copies[-1].start()
    for copy in copies:
        copy.wait()


def add_kernel(parts_ref, after_ref, sent_ref, sent_buf, sem):
    sent_buf[...] = jnp.sum(parts_ref[...].astype(f32), axis=0).astype(bf16)
    copy = pltpu.make_async_copy(sent_buf, sent_ref, sem)
    copy.start()
    copy.wait()


def near_kernel(own_ref, a_ref, b_ref, total_ref):
    total_ref[...] = own_ref[...].astype(f32) + a_ref[...].astype(f32) + b_ref[...].astype(f32)


def column_kernel(near_ref, c_ref, mine_ref, sent_ref, total_ref):
    total_ref[...] = near_ref[...] + c_ref[...].astype(f32)
    side = 1 - lax.axis_index(BLK) // columns
    mine_ref[...] = total_ref[side]
    sent_ref[...] = total_ref[1 - side].astype(bf16)


def final_kernel(group_total, parts_ref, mine_ref, came_ref, weight_out_ref, feature_out_ref):
    feature_out_ref[...] = (mine_ref[...] + came_ref[...].astype(f32)).astype(bf16)
    total = jnp.sum(parts_ref[...].astype(f32), axis=0) * (1.0 / group_total)
    taps, _, width = weight_out_ref.shape
    for tap in range(taps):
        weight_out_ref[tap] = total[:, tap * width : (tap + 1) * width]


def swap(values, axis):
    return lax.ppermute(values, axis, [(0, 1), (1, 0)])


def shards(features, conv_weight, projection, text, labels):
    taps, channels, width = conv_weight.shape
    wide = taps * width
    embed = projection.shape[1]
    half = channels // 2
    quarter = half // 4
    matmul = 2 * clips * cells * channels * wide
    own = jnp.concatenate(
        [
            features.reshape(cells, channels),
            text.reshape(1, channels),
            jnp.broadcast_to(labels.astype(bf16), (15, channels)),
        ]
    )
    copies, extra = call(
        copy_kernel, (shape((clips, cells, channels), bf16), shape((clips, 128), f32))
    )(own)
    group = lax.all_to_all(copies, BLK, 0, 0, axis_index_groups=[blk_order])
    slope, turned, partial = call(
        forward_kernel,
        (
            shape((clips * cells, width), f32),
            shape((2, half, clips * cells), bf16),
            shape((clips, clips, embed + 128), f32),
        ),
        flops=matmul,
    )(group, conv_weight, projection, extra)
    parts = lax.all_to_all(partial, BLK, 0, 0, axis_index_groups=[blk_order])
    grad_text, shifted, sent = call(
        pair_kernel,
        (
            shape((1, embed), f32),
            shape((clips, freq, frames, wide), bf16),
            shape((half, wide), bf16),
        ),
        flops=matmul // 2,
    )(parts, slope, projection, turned)
    kept, *columns_out = call(
        keep_kernel,
        (shape((half, wide), f32),)
        + tuple(shape((2, cells, channels), bf16) for _ in range(columns)),
        scratch=[pltpu.VMEM((2, columns, cells, channels), bf16)],
        flops=matmul + matmul // 2,
    )(turned, shifted, conv_weight)
    came = swap(sent, "core")
    sent = call(
        pair_sum_kernel,
        shape((4, quarter, wide), bf16),
        scratch=[pltpu.VMEM((4, quarter, wide), bf16), DMA((4,))],
        out_specs=HBM,
    )(kept, came)
    parts = lax.all_to_all(sent, NEAR, 0, 0)
    sent = call(
        add_kernel,
        shape((quarter, wide), bf16),
        scratch=[pltpu.VMEM((quarter, wide), bf16), DMA],
        in_specs=[VMEM, pl.BlockSpec(memory_space=pl.ANY)],
        out_specs=HBM,
    )(parts, columns_out[0])
    parts = lax.all_to_all(
        sent.reshape(heights, quarter // heights, wide), FAR, 0, 0, axis_index_groups=[far_order]
    )
    others = [
        lax.ppermute(columns_out[d], BLK, [(i, i ^ d) for i in range(clips)])
        for d in range(1, columns)
    ]
    near = call(near_kernel, shape((2, cells, channels), f32), flops=int(2e10))(
        columns_out[0], others[0], others[2]
    )
    mine, other = call(
        column_kernel,
        (shape((cells, channels), f32), shape((cells, channels), bf16)),
        scratch=[pltpu.VMEM((2, cells, channels), f32)],
        flops=int(3e9),
    )(near, others[1])
    grad_weight, grad_features = call(
        functools.partial(final_kernel, 64),
        (shape((taps, 8, width), f32), shape((cells, channels), bf16)),
    )(parts, mine, lax.ppermute(other, BLK, [(i, i ^ columns) for i in range(clips)]))
    return (
        grad_features.reshape(features.shape),
        grad_weight,
        grad_text.reshape(1, 1, embed),
    )


def solution(mesh):
    fine = Mesh(mesh.devices.reshape(clips, 2, 8, 2, 2), ("blk", "yhi", "z8", "zl", "core"))
    dp = ("yhi", "z8", "zl", "core")
    placed = (
        P(BLK, dp, None, None, None),
        P(None, None, BLK),
        P(BLK, None),
        P(BLK, dp, None),
        P(BLK, dp),
    )
    return jax.shard_map(
        shards,
        mesh=fine,
        in_specs=placed,
        out_specs=(P(BLK, dp, None, None, None), P(None, dp, BLK), P(BLK, dp, None)),
        check_vma=False,
    )
```

```python
import functools

import jax
import jax.numpy as jnp
from jax import lax
from jax.experimental import pallas as pl
from jax.experimental.pallas import tpu as pltpu
from jax.sharding import Mesh, PartitionSpec as P

logit_scale = 10.0
logit_bias = -2.0
loss_scale = 1024.0
norm_eps = 1e-06

BLK = "blk"
NEAR = ("yhi", "zl")
FAR = "z8"
f32 = jnp.float32
bf16 = jnp.bfloat16

clips = 8
freq = 4
frames = 32
cells = freq * frames
columns = 4
last_member = clips - 1
blk_order = [last_member - p for p in range(clips)]
heights = 8
far_order = [5, 4, 3, 2, 1, 0, 7, 6]
vmem_limit = 40 * 1024 * 1024
HBM = pl.BlockSpec(memory_space=pltpu.HBM)
VMEM = pl.BlockSpec(memory_space=pltpu.VMEM)
DMA = pltpu.SemaphoreType.DMA


def shape(dims, dtype):
    return jax.ShapeDtypeStruct(dims, dtype)


def call(kernel, out_shape, scratch=(), flops=0, **specs):
    return pl.pallas_call(
        kernel,
        out_shape=out_shape,
        scratch_shapes=scratch,
        compiler_params=pltpu.CompilerParams(vmem_limit_bytes=vmem_limit),
        cost_estimate=pl.CostEstimate(flops=flops, bytes_accessed=0, transcendentals=0),
        **specs,
    )


def copy_kernel(own_ref, given_ref, copies_ref, label_ref):
    copies_ref[...] = jnp.broadcast_to(own_ref[...][None], copies_ref.shape)
    label_ref[...] = given_ref[...]


def frame_index(count):
    return lax.broadcasted_iota(jnp.int32, (count, 1), 0) % frames


def shift_rows(values, step):
    count = values.shape[0]
    frame = frame_index(count)
    if step == 1:
        return jnp.where(frame == 0, 0.0, pltpu.roll(values, 1, 0))
    return jnp.where(frame == frames - 1, 0.0, pltpu.roll(values, count - 1, 0))


def forward_kernel(
    group_ref,
    weight_ref,
    projection_ref,
    caption_ref,
    label_ref,
    slope_ref,
    turned_ref,
    partial_ref,
):
    inputs = group_ref[...].reshape(clips * cells, -1)
    turned = inputs.T.astype(f32).reshape(2, heights, 2, 2, 8, clips * cells)
    turned = jnp.concatenate([turned[:, z : z + 1] for z in far_order], axis=1)
    block = heights * 8
    for core in range(2):
        for yhi in range(2):
            for zl in range(2):
                rows = turned[yhi, :, zl, core].reshape(block, clips * cells)
                low = (2 * yhi + zl) * block
                turned_ref[core, low : low + block] = rows.astype(bf16)
    out_width = projection_ref.shape[0]
    weight = jnp.concatenate([weight_ref[tap] for tap in range(weight_ref.shape[0])], axis=1)
    products = jnp.dot(inputs, weight, preferred_element_type=f32)
    preact = None
    for a in range(3):
        product = products[:, 3 * a * out_width : 3 * (a + 1) * out_width].reshape(
            clips, freq, frames, 3 * out_width
        )
        low = product[..., :out_width]
        mid = product[..., out_width : 2 * out_width]
        high = product[..., 2 * out_width :]
        bins = []
        for f in range(freq):
            total = mid[:, f]
            if f > 0:
                total = total + low[:, f - 1]
            if f < freq - 1:
                total = total + high[:, f + 1]
            bins.append(total[:, None])
        column = jnp.concatenate(bins, axis=1).reshape(clips * cells, out_width)
        if a == 0:
            column = shift_rows(column, 1)
        if a == 2:
            column = shift_rows(column, -1)
        preact = column if preact is None else preact + column
    sigma = jax.nn.sigmoid(preact)
    slope_ref[...] = sigma * (1.0 + preact * (1.0 - sigma))
    active = (preact * sigma).reshape(clips, cells, out_width)
    pooled = (jnp.sum(active, axis=1) * (1.0 / cells)).astype(bf16)
    partial = jnp.dot(pooled, projection_ref[...], preferred_element_type=f32)
    embed = partial.shape[1]
    partial_ref[:, :, :embed] = jnp.broadcast_to(partial[None], (clips, clips, embed))
    caption = caption_ref[...].astype(f32)
    lanes = partial_ref.shape[2] - embed
    pieces = embed // lanes
    for piece in range(pieces):
        part = caption[:, piece * lanes : (piece + 1) * lanes]
        partial_ref[:, piece : piece + 1, embed:] = jnp.broadcast_to(
            part[None], (clips, 1, lanes)
        )
    partial_ref[:, pieces:, embed:] = jnp.broadcast_to(
        label_ref[pieces:][None], (clips, clips - pieces, lanes)
    )


def row_sum(values):
    return jnp.sum(values, axis=-1, keepdims=True)


def pair_column(audio_unit, caption_row, clip_labels, column):
    logits = logit_scale * row_sum(audio_unit * caption_row) + logit_bias
    signs = jnp.where(clip_labels == column, 1.0, -1.0)
    return -loss_scale * signs * jax.nn.sigmoid(-signs * logits)


def shift_all(pre_grad, shifted_ref):
    width = pre_grad.shape[1]
    zeros = jnp.zeros((clips, frames, width), bf16)
    for a in range(3):
        moved = pre_grad
        if a == 0:
            moved = shift_rows(pre_grad, -1)
        if a == 2:
            moved = shift_rows(pre_grad, 1)
        moved = moved.astype(bf16).reshape(clips, freq, frames, width)
        for b in range(3):
            tap = 3 * a + b
            for f in range(freq):
                source = f - (b - 1)
                block = moved[:, source] if 0 <= source < freq else zeros
                shifted_ref[:, f, :, tap * width : (tap + 1) * width] = block
    return shifted_ref[...].reshape(clips * cells, -1)


def pair_kernel(
    parts_ref,
    slope_ref,
    projection_ref,
    turned_ref,
    text_ref,
    shifted_ref,
    sent_ref,
):
    core = lax.axis_index("core")
    embed = projection_ref.shape[1]
    lanes = parts_ref.shape[2] - embed
    embedding = jnp.sum(parts_ref[:, :, :embed], axis=0)
    inv_audio = lax.rsqrt(row_sum(embedding * embedding) + norm_eps)
    audio_unit = embedding * inv_audio
    clip_labels = jnp.concatenate(
        [parts_ref[c, clips - 1 :, embed : embed + 1] for c in range(clips)], axis=0
    ).astype(jnp.int32)
    member = lax.axis_index(BLK)
    place = last_member - member

    def caption_at(index):
        text_values = jnp.concatenate(
            [parts_ref[index, p : p + 1, embed:] for p in range(embed // lanes)], axis=1
        )
        inv_text = lax.rsqrt(row_sum(text_values * text_values) + norm_eps)
        return text_values * inv_text, inv_text

    audio_grad = jnp.zeros_like(audio_unit)
    for j in range(clips):
        caption, _ = caption_at(j)
        audio_grad = (
            audio_grad + pair_column(audio_unit, caption, clip_labels, last_member - j) * caption
        )
    audio_grad = logit_scale * audio_grad
    caption, inv_text = caption_at(place)
    own_pairs = pair_column(audio_unit, caption, clip_labels, member)
    caption_grad = logit_scale * jnp.sum(own_pairs * audio_unit, axis=0, keepdims=True)
    text_ref[...] = (caption_grad - caption * row_sum(caption * caption_grad)) * inv_text
    embedding_grad = (
        (audio_grad - audio_unit * row_sum(audio_unit * audio_grad)) * inv_audio
    ).astype(bf16)
    pooled_grad = lax.dot_general(
        embedding_grad, projection_ref[...], (((1,), (1,)), ((), ())), preferred_element_type=f32
    )
    width = pooled_grad.shape[1]
    scaled = pooled_grad * (1.0 / cells)
    pre_grad = (scaled[:, None, :] * slope_ref[...].reshape(clips, cells, width)).astype(bf16)
    pre_grad = pre_grad.astype(f32).reshape(clips * cells, width)
    shifted = shift_all(pre_grad, shifted_ref)
    sent_ref[...] = jnp.dot(turned_ref[1 - core], shifted, preferred_element_type=f32).astype(bf16)


def keep_kernel(turned_ref, shifted_ref, weight_ref, kept_ref, *rest):
    out_refs, total_ref = rest[:columns], rest[columns]
    core = lax.axis_index("core")
    shifted = shifted_ref[...].reshape(clips * cells, -1)
    kept_ref[...] = jnp.dot(turned_ref[core], shifted, preferred_element_type=f32)
    weight = jnp.concatenate([weight_ref[tap] for tap in range(weight_ref.shape[0])], axis=1)
    result = lax.dot_general(
        shifted, weight, (((1,), (1,)), ((), ())), preferred_element_type=f32
    )
    total_ref[...] = result.astype(bf16).reshape(total_ref.shape)
    here = lax.axis_index(BLK) % columns
    for d in range(columns):
        out_refs[d][...] = total_ref[:, (columns - 1 - here) ^ d]


def pair_sum_kernel(kept_ref, came_ref, sent_ref, sent_buf, sems):
    copies = []
    count = sent_buf.shape[1]
    for piece in range(sent_buf.shape[0]):
        rows = slice(piece * count, (piece + 1) * count)
        sent_buf[piece] = (kept_ref[rows] + came_ref[rows].astype(f32)).astype(bf16)
        copies.append(
            pltpu.make_async_copy(sent_buf.at[piece], sent_ref.at[piece], sems.at[piece])
        )
        copies[-1].start()
    for copy in copies:
        copy.wait()


def add_kernel(parts_ref, after_ref, sent_ref, sent_buf, sem):
    sent_buf[...] = jnp.sum(parts_ref[...].astype(f32), axis=0).astype(bf16)
    copy = pltpu.make_async_copy(sent_buf, sent_ref, sem)
    copy.start()
    copy.wait()


def near_kernel(own_ref, a_ref, b_ref, total_ref):
    total_ref[...] = own_ref[...].astype(f32) + a_ref[...].astype(f32) + b_ref[...].astype(f32)


def column_kernel(near_ref, c_ref, mine_ref, sent_ref, total_ref):
    total_ref[...] = near_ref[...] + c_ref[...].astype(f32)
    side = 1 - lax.axis_index(BLK) // columns
    mine_ref[...] = total_ref[side]
    sent_ref[...] = total_ref[1 - side].astype(bf16)


def final_kernel(group_total, parts_ref, mine_ref, came_ref, weight_out_ref, feature_out_ref):
    feature_out_ref[...] = (mine_ref[...] + came_ref[...].astype(f32)).astype(bf16)
    total = jnp.sum(parts_ref[...].astype(f32), axis=0) * (1.0 / group_total)
    taps, _, width = weight_out_ref.shape
    for tap in range(taps):
        weight_out_ref[tap] = total[:, tap * width : (tap + 1) * width]


def swap(values, axis):
    return lax.ppermute(values, axis, [(0, 1), (1, 0)])


def shards(features, conv_weight, projection, text, labels):
    taps, channels, width = conv_weight.shape
    wide = taps * width
    embed = projection.shape[1]
    half = channels // 2
    quarter = half // 4
    matmul = 2 * clips * cells * channels * wide
    copies, label = call(
        copy_kernel, (shape((clips, cells, channels), bf16), shape((clips, 128), f32))
    )(features.reshape(cells, channels), jnp.broadcast_to(labels.astype(f32), (clips, 128)))
    group = lax.all_to_all(copies, BLK, 0, 0, axis_index_groups=[blk_order])
    slope, turned, partial = call(
        forward_kernel,
        (
            shape((clips * cells, width), f32),
            shape((2, half, clips * cells), bf16),
            shape((clips, clips, embed + 128), f32),
        ),
        flops=matmul,
    )(group, conv_weight, projection, text.reshape(1, embed), label)
    parts = lax.all_to_all(partial, BLK, 0, 0, axis_index_groups=[blk_order])
    grad_text, shifted, sent = call(
        pair_kernel,
        (
            shape((1, embed), f32),
            shape((clips, freq, frames, wide), bf16),
            shape((half, wide), bf16),
        ),
        flops=matmul // 2,
    )(parts, slope, projection, turned)
    kept, *columns_out = call(
        keep_kernel,
        (shape((half, wide), f32),)
        + tuple(shape((2, cells, channels), bf16) for _ in range(columns)),
        scratch=[pltpu.VMEM((2, columns, cells, channels), bf16)],
        flops=matmul + matmul // 2,
    )(turned, shifted, conv_weight)
    came = swap(sent, "core")
    sent = call(
        pair_sum_kernel,
        shape((4, quarter, wide), bf16),
        scratch=[pltpu.VMEM((4, quarter, wide), bf16), DMA((4,))],
        out_specs=HBM,
    )(kept, came)
    parts = lax.all_to_all(sent, NEAR, 0, 0)
    sent = call(
        add_kernel,
        shape((quarter, wide), bf16),
        scratch=[pltpu.VMEM((quarter, wide), bf16), DMA],
        in_specs=[VMEM, pl.BlockSpec(memory_space=pl.ANY)],
        out_specs=HBM,
    )(parts, columns_out[0])
    parts = lax.all_to_all(
        sent.reshape(heights, quarter // heights, wide), FAR, 0, 0, axis_index_groups=[far_order]
    )
    others = [
        lax.ppermute(columns_out[d], BLK, [(i, i ^ d) for i in range(clips)])
        for d in range(1, columns)
    ]
    near = call(near_kernel, shape((2, cells, channels), f32), flops=int(2e10))(
        columns_out[0], others[0], others[2]
    )
    mine, other = call(
        column_kernel,
        (shape((cells, channels), f32), shape((cells, channels), bf16)),
        scratch=[pltpu.VMEM((2, cells, channels), f32)],
        flops=int(3e9),
    )(near, others[1])
    grad_weight, grad_features = call(
        functools.partial(final_kernel, 64),
        (shape((taps, 8, width), f32), shape((cells, channels), bf16)),
    )(parts, mine, lax.ppermute(other, BLK, [(i, i ^ columns) for i in range(clips)]))
    return (
        grad_features.reshape(features.shape),
        grad_weight,
        grad_text.reshape(1, 1, embed),
    )


def solution(mesh):
    fine = Mesh(mesh.devices.reshape(clips, 2, 8, 2, 2), ("blk", "yhi", "z8", "zl", "core"))
    dp = ("yhi", "z8", "zl", "core")
    placed = (
        P(BLK, dp, None, None, None),
        P(None, None, BLK),
        P(BLK, None),
        P(BLK, dp, None),
        P(BLK, dp),
    )
    return jax.shard_map(
        shards,
        mesh=fine,
        in_specs=placed,
        out_specs=(P(BLK, dp, None, None, None), P(None, dp, BLK), P(BLK, dp, None)),
        check_vma=False,
    )
```

```python
import functools

import jax
import jax.numpy as jnp
from jax import lax
from jax.experimental import pallas as pl
from jax.experimental.pallas import tpu as pltpu
from jax.sharding import Mesh, PartitionSpec as P

logit_scale = 10.0
logit_bias = -2.0
loss_scale = 1024.0
norm_eps = 1e-06

BLK = "blk"
NEAR = ("yhi", "zl")
FAR = "z8"
f32 = jnp.float32
bf16 = jnp.bfloat16

clips = 8
freq = 4
frames = 32
cells = freq * frames
columns = 4
last_member = clips - 1
blk_order = [last_member - p for p in range(clips)]
gather_order = [6, 7, 5, 4, 2, 3, 1, 0]
heights = 8
far_order = [5, 4, 3, 2, 1, 0, 7, 6]
vmem_limit = 40 * 1024 * 1024
HBM = pl.BlockSpec(memory_space=pltpu.HBM)
VMEM = pl.BlockSpec(memory_space=pltpu.VMEM)
DMA = pltpu.SemaphoreType.DMA


def shape(dims, dtype):
    return jax.ShapeDtypeStruct(dims, dtype)


def call(kernel, out_shape, scratch=(), flops=0, **specs):
    return pl.pallas_call(
        kernel,
        out_shape=out_shape,
        scratch_shapes=scratch,
        compiler_params=pltpu.CompilerParams(vmem_limit_bytes=vmem_limit),
        cost_estimate=pl.CostEstimate(flops=flops, bytes_accessed=0, transcendentals=0),
        **specs,
    )


def copy_kernel(own_ref, given_ref, copies_ref, label_ref):
    copies_ref[...] = jnp.broadcast_to(own_ref[...][None], copies_ref.shape)
    label_ref[...] = given_ref[...]


def frame_index(count):
    return lax.broadcasted_iota(jnp.int32, (count, 1), 0) % frames


def shift_rows(values, step):
    count = values.shape[0]
    frame = frame_index(count)
    if step == 1:
        return jnp.where(frame == 0, 0.0, pltpu.roll(values, 1, 0))
    return jnp.where(frame == frames - 1, 0.0, pltpu.roll(values, count - 1, 0))


def forward_kernel(
    group_ref,
    weight_ref,
    projection_ref,
    caption_ref,
    label_ref,
    slope_ref,
    turned_ref,
    partial_ref,
):
    inputs = jnp.concatenate([group_ref[gather_order.index(member)] for member in blk_order])
    turned = inputs.T.astype(f32).reshape(2, heights, 2, 2, 8, clips * cells)
    turned = jnp.concatenate([turned[:, z : z + 1] for z in far_order], axis=1)
    block = heights * 8
    for core in range(2):
        for yhi in range(2):
            for zl in range(2):
                rows = turned[yhi, :, zl, core].reshape(block, clips * cells)
                low = (2 * yhi + zl) * block
                turned_ref[core, low : low + block] = rows.astype(bf16)
    out_width = projection_ref.shape[0]
    weight = jnp.concatenate([weight_ref[tap] for tap in range(weight_ref.shape[0])], axis=1)
    products = jnp.dot(inputs, weight, preferred_element_type=f32)
    preact = None
    for a in range(3):
        product = products[:, 3 * a * out_width : 3 * (a + 1) * out_width].reshape(
            clips, freq, frames, 3 * out_width
        )
        low = product[..., :out_width]
        mid = product[..., out_width : 2 * out_width]
        high = product[..., 2 * out_width :]
        bins = []
        for f in range(freq):
            total = mid[:, f]
            if f > 0:
                total = total + low[:, f - 1]
            if f < freq - 1:
                total = total + high[:, f + 1]
            bins.append(total[:, None])
        column = jnp.concatenate(bins, axis=1).reshape(clips * cells, out_width)
        if a == 0:
            column = shift_rows(column, 1)
        if a == 2:
            column = shift_rows(column, -1)
        preact = column if preact is None else preact + column
    sigma = jax.nn.sigmoid(preact)
    slope_ref[...] = sigma * (1.0 + preact * (1.0 - sigma))
    active = (preact * sigma).reshape(clips, cells, out_width)
    pooled = (jnp.sum(active, axis=1) * (1.0 / cells)).astype(bf16)
    partial = jnp.dot(pooled, projection_ref[...], preferred_element_type=f32)
    embed = partial.shape[1]
    partial_ref[:, :, :embed] = jnp.broadcast_to(partial[None], (clips, clips, embed))
    caption = caption_ref[...].astype(f32)
    lanes = partial_ref.shape[2] - embed
    pieces = embed // lanes
    for piece in range(pieces):
        part = caption[:, piece * lanes : (piece + 1) * lanes]
        partial_ref[:, piece : piece + 1, embed:] = jnp.broadcast_to(
            part[None], (clips, 1, lanes)
        )
    partial_ref[:, pieces:, embed:] = jnp.broadcast_to(
        label_ref[pieces:][None], (clips, clips - pieces, lanes)
    )


def row_sum(values):
    return jnp.sum(values, axis=-1, keepdims=True)


def pair_column(audio_unit, caption_row, clip_labels, column):
    logits = logit_scale * row_sum(audio_unit * caption_row) + logit_bias
    signs = jnp.where(clip_labels == column, 1.0, -1.0)
    return -loss_scale * signs * jax.nn.sigmoid(-signs * logits)


def shift_all(pre_grad, shifted_ref):
    width = pre_grad.shape[1]
    zeros = jnp.zeros((clips, frames, width), bf16)
    for a in range(3):
        moved = pre_grad
        if a == 0:
            moved = shift_rows(pre_grad, -1)
        if a == 2:
            moved = shift_rows(pre_grad, 1)
        moved = moved.astype(bf16).reshape(clips, freq, frames, width)
        for b in range(3):
            tap = 3 * a + b
            for f in range(freq):
                source = f - (b - 1)
                block = moved[:, source] if 0 <= source < freq else zeros
                shifted_ref[:, f, :, tap * width : (tap + 1) * width] = block
    return shifted_ref[...].reshape(clips * cells, -1)


def pair_kernel(
    parts_ref,
    slope_ref,
    projection_ref,
    turned_ref,
    text_ref,
    shifted_ref,
    sent_ref,
):
    core = lax.axis_index("core")
    embed = projection_ref.shape[1]
    lanes = parts_ref.shape[2] - embed
    embedding = jnp.sum(parts_ref[:, :, :embed], axis=0)
    inv_audio = lax.rsqrt(row_sum(embedding * embedding) + norm_eps)
    audio_unit = embedding * inv_audio
    clip_labels = jnp.concatenate(
        [parts_ref[c, clips - 1 :, embed : embed + 1] for c in range(clips)], axis=0
    ).astype(jnp.int32)
    member = lax.axis_index(BLK)
    place = last_member - member

    def caption_at(index):
        text_values = jnp.concatenate(
            [parts_ref[index, p : p + 1, embed:] for p in range(embed // lanes)], axis=1
        )
        inv_text = lax.rsqrt(row_sum(text_values * text_values) + norm_eps)
        return text_values * inv_text, inv_text

    audio_grad = jnp.zeros_like(audio_unit)
    for j in range(clips):
        caption, _ = caption_at(j)
        audio_grad = (
            audio_grad + pair_column(audio_unit, caption, clip_labels, last_member - j) * caption
        )
    audio_grad = logit_scale * audio_grad
    caption, inv_text = caption_at(place)
    own_pairs = pair_column(audio_unit, caption, clip_labels, member)
    caption_grad = logit_scale * jnp.sum(own_pairs * audio_unit, axis=0, keepdims=True)
    text_ref[...] = (caption_grad - caption * row_sum(caption * caption_grad)) * inv_text
    embedding_grad = (
        (audio_grad - audio_unit * row_sum(audio_unit * audio_grad)) * inv_audio
    ).astype(bf16)
    pooled_grad = lax.dot_general(
        embedding_grad, projection_ref[...], (((1,), (1,)), ((), ())), preferred_element_type=f32
    )
    width = pooled_grad.shape[1]
    scaled = pooled_grad * (1.0 / cells)
    pre_grad = (scaled[:, None, :] * slope_ref[...].reshape(clips, cells, width)).astype(bf16)
    pre_grad = pre_grad.astype(f32).reshape(clips * cells, width)
    shifted = shift_all(pre_grad, shifted_ref)
    sent_ref[...] = jnp.dot(turned_ref[1 - core], shifted, preferred_element_type=f32).astype(bf16)


def keep_kernel(turned_ref, shifted_ref, weight_ref, kept_ref, *rest):
    out_refs, total_ref = rest[:columns], rest[columns]
    core = lax.axis_index("core")
    shifted = shifted_ref[...].reshape(clips * cells, -1)
    kept_ref[...] = jnp.dot(turned_ref[core], shifted, preferred_element_type=f32)
    weight = jnp.concatenate([weight_ref[tap] for tap in range(weight_ref.shape[0])], axis=1)
    result = lax.dot_general(
        shifted, weight, (((1,), (1,)), ((), ())), preferred_element_type=f32
    )
    total_ref[...] = result.astype(bf16).reshape(total_ref.shape)
    here = lax.axis_index(BLK) % columns
    for d in range(columns):
        out_refs[d][...] = total_ref[:, (columns - 1 - here) ^ d]


def pair_sum_kernel(kept_ref, came_ref, sent_ref, sent_buf, sems):
    copies = []
    count = sent_buf.shape[1]
    for piece in range(sent_buf.shape[0]):
        rows = slice(piece * count, (piece + 1) * count)
        sent_buf[piece] = (kept_ref[rows] + came_ref[rows].astype(f32)).astype(bf16)
        copies.append(
            pltpu.make_async_copy(sent_buf.at[piece], sent_ref.at[piece], sems.at[piece])
        )
        copies[-1].start()
    for copy in copies:
        copy.wait()


def add_kernel(parts_ref, after_ref, sent_ref, sent_buf, sem):
    sent_buf[...] = jnp.sum(parts_ref[...].astype(f32), axis=0).astype(bf16)
    copy = pltpu.make_async_copy(sent_buf, sent_ref, sem)
    copy.start()
    copy.wait()


def near_kernel(own_ref, a_ref, b_ref, total_ref):
    total_ref[...] = own_ref[...].astype(f32) + a_ref[...].astype(f32) + b_ref[...].astype(f32)


def column_kernel(near_ref, c_ref, mine_ref, sent_ref, total_ref):
    total_ref[...] = near_ref[...] + c_ref[...].astype(f32)
    side = 1 - lax.axis_index(BLK) // columns
    mine_ref[...] = total_ref[side]
    sent_ref[...] = total_ref[1 - side].astype(bf16)


def final_kernel(group_total, parts_ref, mine_ref, came_ref, weight_out_ref, feature_out_ref):
    feature_out_ref[...] = (mine_ref[...] + came_ref[...].astype(f32)).astype(bf16)
    total = jnp.sum(parts_ref[...].astype(f32), axis=0) * (1.0 / group_total)
    taps, _, width = weight_out_ref.shape
    for tap in range(taps):
        weight_out_ref[tap] = total[:, tap * width : (tap + 1) * width]


def swap(values, axis):
    return lax.ppermute(values, axis, [(0, 1), (1, 0)])


def shards(features, conv_weight, projection, text, labels):
    taps, channels, width = conv_weight.shape
    wide = taps * width
    embed = projection.shape[1]
    half = channels // 2
    quarter = half // 4
    matmul = 2 * clips * cells * channels * wide
    copies, label = call(
        copy_kernel, (shape((clips, cells, channels), bf16), shape((clips, 128), f32))
    )(features.reshape(cells, channels), jnp.broadcast_to(labels.astype(f32), (clips, 128)))
    group = lax.all_to_all(copies, BLK, 0, 0, axis_index_groups=[gather_order])
    slope, turned, partial = call(
        forward_kernel,
        (
            shape((clips * cells, width), f32),
            shape((2, half, clips * cells), bf16),
            shape((clips, clips, embed + 128), f32),
        ),
        flops=matmul,
    )(group, conv_weight, projection, text.reshape(1, embed), label)
    parts = lax.all_to_all(partial, BLK, 0, 0, axis_index_groups=[blk_order])
    grad_text, shifted, sent = call(
        pair_kernel,
        (
            shape((1, embed), f32),
            shape((clips, freq, frames, wide), bf16),
            shape((half, wide), bf16),
        ),
        flops=matmul // 2,
    )(parts, slope, projection, turned)
    kept, *columns_out = call(
        keep_kernel,
        (shape((half, wide), f32),)
        + tuple(shape((2, cells, channels), bf16) for _ in range(columns)),
        scratch=[pltpu.VMEM((2, columns, cells, channels), bf16)],
        flops=matmul + matmul // 2,
    )(turned, shifted, conv_weight)
    came = swap(sent, "core")
    sent = call(
        pair_sum_kernel,
        shape((4, quarter, wide), bf16),
        scratch=[pltpu.VMEM((4, quarter, wide), bf16), DMA((4,))],
        out_specs=HBM,
    )(kept, came)
    parts = lax.all_to_all(sent, NEAR, 0, 0)
    sent = call(
        add_kernel,
        shape((quarter, wide), bf16),
        scratch=[pltpu.VMEM((quarter, wide), bf16), DMA],
        in_specs=[VMEM, pl.BlockSpec(memory_space=pl.ANY)],
        out_specs=HBM,
    )(parts, columns_out[0])
    parts = lax.all_to_all(
        sent.reshape(heights, quarter // heights, wide), FAR, 0, 0, axis_index_groups=[far_order]
    )
    others = [
        lax.ppermute(columns_out[d], BLK, [(i, i ^ d) for i in range(clips)])
        for d in range(1, columns)
    ]
    near = call(near_kernel, shape((2, cells, channels), f32), flops=int(2e10))(
        columns_out[0], others[0], others[2]
    )
    mine, other = call(
        column_kernel,
        (shape((cells, channels), f32), shape((cells, channels), bf16)),
        scratch=[pltpu.VMEM((2, cells, channels), f32)],
        flops=int(3e9),
    )(near, others[1])
    grad_weight, grad_features = call(
        functools.partial(final_kernel, 64),
        (shape((taps, 8, width), f32), shape((cells, channels), bf16)),
    )(parts, mine, lax.ppermute(other, BLK, [(i, i ^ columns) for i in range(clips)]))
    return (
        grad_features.reshape(features.shape),
        grad_weight,
        grad_text.reshape(1, 1, embed),
    )


def solution(mesh):
    fine = Mesh(mesh.devices.reshape(clips, 2, 8, 2, 2), ("blk", "yhi", "z8", "zl", "core"))
    dp = ("yhi", "z8", "zl", "core")
    placed = (
        P(BLK, dp, None, None, None),
        P(None, None, BLK),
        P(BLK, None),
        P(BLK, dp, None),
        P(BLK, dp),
    )
    return jax.shard_map(
        shards,
        mesh=fine,
        in_specs=placed,
        out_specs=(P(BLK, dp, None, None, None), P(None, dp, BLK), P(BLK, dp, None)),
        check_vma=False,
    )
```
